32 devices in a mesh: seq: 8 (over y, x, core), head: 4 (over z).
Axes of the slice: x: 2, y: 2, z: 4, core: 2. Of those that a mesh axis runs over, the one named last changes fastest.
Arguments:
- queries: bfloat16 [32, 2048, 128], P('head', 'seq'), may hold values from -0.5390625 to 0.5390625
- keys: bfloat16 [32, 2048, 128], P('head', 'seq'), may hold values from -0.5390625 to 0.5390625
- values: bfloat16 [32, 2048, 128], P('head', 'seq'), may hold values from -15 to 15
- log_decay: float32 [32, 2048], P('head', 'seq'), may hold values from -1 to 0, as said below
- level_weight: float32 [32, 21, 2048], P('head', None, 'seq'), may hold values from 0.2 to 2
- gate_input: bfloat16 [32, 2048, 128], P('head', 'seq'), may hold values from -6 to 6
- norm_gain: float32 [32, 128], P('head'), may hold values from 0.5 to 1.5
- out_grad: bfloat16 [32, 2048, 128], P('head', 'seq'), may hold values from -15 to 15
Outputs:
- layer_out: bfloat16 [32, 2048, 128], P('head', 'seq')
- grad_queries: bfloat16 [32, 2048, 128], P('head', 'seq')
- grad_keys: bfloat16 [32, 2048, 128], P('head', 'seq')
- grad_values: bfloat16 [32, 2048, 128], P('head', 'seq')
- grad_levels: float32 [32, 21, 2048], P('head', None, 'seq')
- grad_gate: bfloat16 [32, 2048, 128], P('head', 'seq')
- grad_gain: float32 [32, 128], P('head')
The draws below stay inside these ranges and needn't reach their ends.
Inputs may be any that keep to these rules, and one draw needn't show every extreme that they name: `log_decay`: negative logarithms of decays.
All inputs are finite; a program needn't handle non-finite values.
Results may differ from the reference program's by a relative error of at most 0.0051.
Values sent between devices are 32-bit elements; how exact they have to be, the bound alone decides.
A program may use at most 64 MiB of HBM per device.

```python
import math
import jax
import jax.numpy as jnp
from jax import lax

HEADS = 32
STATE = 128
HEAD_DIM = 128
LEVELS = 21
C_DEV = 256
TOKENS = 2048
N_SEQ = 8


def draw_log_decay(key, part):
    keys = jax.random.split(jax.random.fold_in(key, 11), 7)
    blocks = TOKENS // C_DEV
    share = 0.5
    quick = jax.random.uniform(keys[0], (HEADS, 1)) < share
    quick_rate = jnp.exp(jax.random.uniform(keys[1], (HEADS, 1), minval=jnp.log(1.0 / 50.0), maxval=jnp.log(1.0 / 30.0)))
    slow_rate = jax.random.uniform(keys[2], (HEADS, 1), minval=0.2, maxval=0.8) / TOKENS
    decay_speed = jnp.where(quick, quick_rate, slow_rate)
    multiplier_term = jnp.exp(jax.random.uniform(keys[3], (HEADS, blocks), minval=-0.7, maxval=0.7))
    multiplier_term = jnp.repeat(multiplier_term, C_DEV, axis=1)
    coarse_estimate = jax.random.uniform(keys[4], (HEADS, TOKENS), minval=0.5, maxval=1.5)
    spots = jax.random.randint(keys[5], (3,), 0, TOKENS)
    gate_intensity = jnp.log(jax.random.uniform(keys[6], (3,), minval=0.5, maxval=0.8))
    positioned_rows = jnp.arange(TOKENS)[None, :] == spots[:, None]
    spike_level = jnp.sum(jnp.where(positioned_rows, gate_intensity[:, None], 0.0), axis=0)
    value_entry = -decay_speed * multiplier_term * coarse_estimate + spike_level[None, :]
    return jnp.clip(value_entry, -1.0, -1e-07).astype(jnp.float32)


def draw_values(key, part):
    keys = jax.random.split(jax.random.fold_in(key, 23), 1)
    rising = 1.0 + 2.0 * jnp.arange(HEADS, dtype=jnp.float32)[:, None, None] / max(HEADS - 1, 1)
    base = jnp.clip(jax.random.normal(keys[0], (HEADS, TOKENS, HEAD_DIM)), -5.0, 5.0)
    return (base * rising).astype(jnp.bfloat16)


def draw_out_grad(key, part):
    keys = jax.random.split(jax.random.fold_in(key, 37), 1)
    rising = 1.0 + 2.0 * jnp.arange(TOKENS, dtype=jnp.float32)[None, :, None] / TOKENS
    base = jnp.clip(jax.random.normal(keys[0], (HEADS, TOKENS, HEAD_DIM)), -5.0, 5.0)
    return (base * rising).astype(jnp.bfloat16)


def shard_levels(rng, extent, shards, low, high):
    loudness = 1.0
    for dim, blocks in shards:
        draws = jax.random.uniform(jax.random.fold_in(jax.random.fold_in(rng, 6), dim), (blocks,), jnp.float32, low / len(shards), high / len(shards))
        loudness = loudness * jnp.repeat(jnp.exp(draws), extent[dim] // blocks).reshape((-1,) + (1,) * (len(extent) - 1 - dim))
    return loudness


def bell_draw(own_key, dims, scale, most, shards=(), kind=jnp.bfloat16):
    level = shard_levels(own_key, dims, shards, -0.22, 0.18) if shards else 1.0
    drawn = jax.random.normal(own_key, dims, jnp.float32) * scale * level
    return jnp.minimum(jnp.maximum(drawn, -most), most).astype(kind)


def setup_inputs(seed: int = 0) -> dict:
    seeds = jax.random.split(jax.random.key(seed), 9)
    return {
        "queries": bell_draw(seeds[0], (HEADS, TOKENS, STATE), 0.09, 0.5390625, ((0, 4), (1, 8))),
        "keys": bell_draw(seeds[1], (HEADS, TOKENS, STATE), 0.09, 0.5390625, ((0, 4), (1, 8))),
        "values": draw_values(jax.random.fold_in(seeds[8], 71), 0),
        "log_decay": draw_log_decay(jax.random.fold_in(seeds[8], 71), 0),
        "level_weight": jnp.clip(jnp.exp(math.log(2.0) - 2.3025851 * jax.random.uniform(seeds[4], (HEADS, LEVELS, TOKENS), jnp.float32) ** shard_levels(seeds[4], (HEADS, LEVELS, TOKENS), ((0, 4), (2, 8)), -0.2, 0.2)), 0.2, 2.0),
        "gate_input": bell_draw(seeds[5], (HEADS, TOKENS, HEAD_DIM), 1.0, 6.0, ((0, 4), (1, 8))),
        "norm_gain": jnp.clip(1.0 + 0.1 * jax.random.normal(seeds[6], (HEADS, HEAD_DIM), jnp.float32), 0.5, 1.5),
        "out_grad": draw_out_grad(jax.random.fold_in(seeds[8], 71), 0),
    }


EPSILON = 1e-05
HIGH = lax.Precision.HIGHEST

def level_table(row_start, rows, width, depth):
    row_ids = row_start + lax.iota(jnp.int32, rows)
    column_ids = lax.iota(jnp.int32, width)
    crossed = jnp.bitwise_xor(row_ids[:, None], column_ids[None, :])
    level = jnp.zeros((rows, width), jnp.int32)
    for shift in range(depth):
        level = level + (jnp.right_shift(crossed, shift) > 0).astype(jnp.int32)
    causal = column_ids[None, :] <= row_ids[:, None]
    return (level, causal)

def pair_weights(running, mix_rows, row_start, rows, depth):
    level, causal = level_table(row_start, rows, running.shape[1], depth)
    run_rows = lax.dynamic_slice_in_dim(running, row_start, rows, 1)
    spread = jnp.where(causal[None], run_rows[:, :, None] - running[:, None, :], 0.0)
    decay = jnp.where(causal[None], jnp.exp(spread), 0.0)
    chosen = jnp.zeros_like(decay)
    for place in range(depth + 1):
        chosen = chosen + jnp.where((level == place)[None], mix_rows[:, place, :, None], 0.0)
    return (decay, chosen, level)

def intra_forward(queries, keys, values, running, mix, depth):
    heads, width, state = queries.shape
    rows = min(width, 512)

    def one_block(index):
        start = index * rows
        q_rows = lax.dynamic_slice_in_dim(queries, start, rows, 1)
        mix_rows = lax.dynamic_slice_in_dim(mix, start, rows, 2)
        decay, chosen, level = pair_weights(running, mix_rows, start, rows, depth)
        scores = jnp.einsum('hik,hjk->hij', q_rows.astype(jnp.float32), keys.astype(jnp.float32))
        mixing = (scores * decay * chosen).astype(jnp.bfloat16)
        return jnp.einsum('hij,hjp->hip', mixing.astype(jnp.float32), values.astype(jnp.float32))
    blocks = lax.map(one_block, jnp.arange(width // rows, dtype=jnp.int32))
    return jnp.moveaxis(blocks, 0, 1).reshape(heads, width, -1)

def intra_backward(queries, keys, values, running, mix, grad_mixed, depth):
    heads, width, state = queries.shape
    rows = min(width, 512)
    grad_wide = grad_mixed.astype(jnp.float32)
    keys_wide = keys.astype(jnp.float32)
    values_wide = values.astype(jnp.float32)

    def one_block(carry, index):
        grad_keys, grad_values = carry
        start = index * rows
        q_rows = lax.dynamic_slice_in_dim(queries, start, rows, 1).astype(jnp.float32)
        g_rows = lax.dynamic_slice_in_dim(grad_wide, start, rows, 1)
        mix_rows = lax.dynamic_slice_in_dim(mix, start, rows, 2)
        decay, chosen, level = pair_weights(running, mix_rows, start, rows, depth)
        scores = jnp.einsum('hik,hjk->hij', q_rows, keys_wide)
        weight = decay * chosen
        mixing = (scores * weight).astype(jnp.bfloat16).astype(jnp.float32)
        grad_mixing = jnp.einsum('hip,hjp->hij', g_rows, values_wide)
        grad_scores = (grad_mixing * weight).astype(jnp.bfloat16).astype(jnp.float32)
        grad_q_rows = jnp.einsum('hij,hjk->hik', grad_scores, keys_wide)
        grad_keys = grad_keys + jnp.einsum('hij,hik->hjk', grad_scores, q_rows)
        grad_values = grad_values + jnp.einsum('hij,hip->hjp', mixing, g_rows)
        moved = grad_mixing * scores * decay
        per_level = jnp.stack([lax.optimization_barrier(jnp.sum(jnp.where((level == place)[None], moved, 0.0), axis=2)) for place in range(depth + 1)], axis=1)
        return ((grad_keys, grad_values), (grad_q_rows, per_level))
    start_carry = (jnp.zeros((heads, width, state), jnp.float32), jnp.zeros((heads, width, values.shape[2]), jnp.float32))
    (grad_keys, grad_values), (q_blocks, level_blocks) = lax.scan(one_block, start_carry, jnp.arange(width // rows, dtype=jnp.int32))
    grad_queries = jnp.moveaxis(q_blocks, 0, 1).reshape(heads, width, state)
    grad_levels = jnp.moveaxis(level_blocks, 0, 2).reshape(heads, depth + 1, width)
    return (grad_queries, grad_keys, grad_values, grad_levels)

def route_weights(late, early, before, through, levels):
    spread = before[:, None, :] - through[None, :, :]
    result = []
    for place in range(levels):
        span = 2 ** place
        inside = (late[:, None] // span % 2 == 1) & (early[None, :] // span % 2 == 0) & (late[:, None] // (2 * span) == early[None, :] // (2 * span))
        inside = inside[:, :, None]
        result.append(jnp.where(inside, jnp.exp(jnp.where(inside, spread, 0.0)), 0.0))
    return jnp.stack(result, axis=0)

def reference(queries, keys, values, log_decay, level_weight, gate_input, norm_gain, out_grad):
    heads = queries.shape[0]
    count = N_SEQ
    width = C_DEV
    depth = width.bit_length() - 1
    levels_dev = count.bit_length() - 1

    def stretched(array):
        return jnp.moveaxis(array.reshape((heads, count, width) + array.shape[2:]), 1, 0)

    def joined(array):
        return jnp.moveaxis(array, 0, 1).reshape((heads, count * width) + array.shape[3:])
    q_parts = stretched(queries)
    k_parts = stretched(keys)
    v_parts = stretched(values)
    running = jnp.cumsum(stretched(log_decay), axis=2)
    mixes = jnp.moveaxis(level_weight.reshape(heads, LEVELS, count, width), 2, 0)
    intra_mix = mixes[:, :, :depth + 1]
    inter_mix = mixes[:, :, depth + 1:depth + 1 + levels_dev]
    inner = lax.map(lambda item: intra_forward(item[0], item[1], item[2], item[3], item[4], depth), (q_parts, k_parts, v_parts, running, intra_mix))
    tail = jnp.exp(running[:, :, -1:] - running)
    states = lax.map(lambda item: jnp.einsum('hjk,hjp->hkp', item[0].astype(jnp.float32) * item[2][:, :, None], item[1].astype(jnp.float32), precision=HIGH), (k_parts, v_parts, tail))
    totals = running[:, :, -1]
    through = jnp.cumsum(totals, axis=0)
    before = through - totals
    stretch_ids = jnp.arange(count, dtype=jnp.int32)

    def gather_buckets(index):
        weights = route_weights(index[None], stretch_ids, lax.dynamic_index_in_dim(before, index, 0), through, levels_dev)[:, 0]
        return jnp.einsum('ljh,jhkp->lhkp', weights, states, precision=HIGH)
    buckets = lax.map(gather_buckets, stretch_ids)
    reach = inter_mix * jnp.exp(running)[:, :, None, :]

    def outer_part(item):
        through_q = jnp.einsum('hik,lhkp->lhip', item[0].astype(jnp.float32), item[1], precision=HIGH)
        return jnp.einsum('hli,lhip->hip', item[2], through_q, precision=HIGH)
    outer = lax.map(outer_part, (q_parts, buckets, reach))
    mixed = inner + outer
    gate = stretched(gate_input).astype(jnp.float32)
    sigmoid_gate = jax.nn.sigmoid(gate)
    gate_act = gate * sigmoid_gate
    gated = mixed * gate_act
    total = HEADS * HEAD_DIM
    inverse = lax.rsqrt(lax.optimization_barrier(jnp.sum(gated * gated, axis=(1, 3))) / total + EPSILON)[:, None, :, None]
    gain = norm_gain[None, :, None, :]
    layer_out = (gain * gated * inverse).astype(jnp.bfloat16)
    grad_y = stretched(out_grad).astype(jnp.float32)
    scaled = grad_y * gain
    cross = lax.optimization_barrier(jnp.sum(gated * scaled, axis=(1, 3)))[:, None, :, None]
    grad_gated = inverse * scaled - gated * (inverse * inverse * inverse * cross / total)
    grad_gain = lax.optimization_barrier(jnp.sum(grad_y * gated * inverse, axis=(0, 2)))
    grad_gate = (grad_gated * mixed * sigmoid_gate * (1.0 + gate * (1.0 - sigmoid_gate))).astype(jnp.bfloat16)
    grad_mixed = (grad_gated * gate_act).astype(jnp.bfloat16)
    gq_in, gk_in, gv_in, glev_in = lax.map(lambda item: intra_backward(item[0], item[1], item[2], item[3], item[4], item[5], depth), (q_parts, k_parts, v_parts, running, intra_mix, grad_mixed))

    def inter_back(item):
        q_wide = item[0].astype(jnp.float32)
        grad_wide = item[1].astype(jnp.float32)
        bucket, reach_here, run_here = (item[2], item[3], item[4])
        through_q = jnp.einsum('hik,lhkp->lhip', q_wide, bucket, precision=HIGH)
        grad_levels_here = jnp.exp(run_here)[:, None, :] * jnp.einsum('lhip,hip->hli', through_q, grad_wide, precision=HIGH)
        scaled_q = reach_here[:, :, :, None] * q_wide[:, None]
        bucket_grads = jnp.einsum('hlik,hip->lhkp', scaled_q, grad_wide, precision=HIGH)
        pulled = jnp.einsum('lhkp,hip->lhik', bucket, grad_wide, precision=HIGH)
        grad_q_here = jnp.einsum('hli,lhik->hik', reach_here, pulled, precision=HIGH)
        return (grad_q_here, grad_levels_here, bucket_grads)
    gq_out, glev_out, bucket_grads = lax.map(inter_back, (q_parts, grad_mixed, buckets, reach, running))

    def gather_grads(index):
        weights = route_weights(stretch_ids, index[None], before, lax.dynamic_index_in_dim(through, index, 0), levels_dev)[:, :, 0]
        return jnp.einsum('lch,clhkp->hkp', weights, bucket_grads, precision=HIGH)
    state_grads = lax.map(gather_grads, stretch_ids)
    gk_out = tail[..., None] * jnp.einsum('chkp,chjp->chjk', state_grads, v_parts.astype(jnp.float32), precision=HIGH)
    gv_out = tail[..., None] * jnp.einsum('chkp,chjk->chjp', state_grads, k_parts.astype(jnp.float32), precision=HIGH)
    rest = LEVELS - depth - 1 - levels_dev
    level_parts = jnp.concatenate([glev_in, glev_out, jnp.zeros((count, heads, rest, width), jnp.float32)], axis=2)
    grad_levels = jnp.moveaxis(level_parts, 0, 2).reshape(heads, LEVELS, count * width)
    return (joined(layer_out), joined((gq_in + gq_out).astype(jnp.bfloat16)), joined((gk_in + gk_out).astype(jnp.bfloat16)), joined((gv_in + gv_out).astype(jnp.bfloat16)), grad_levels, joined(grad_gate), grad_gain)
```

```python
import functools

import jax
import jax.numpy as jnp
from jax import lax
from jax.experimental import pallas as pl
from jax.experimental.pallas import tpu as pltpu
from jax.sharding import PartitionSpec as P

EPSILON = 1e-05
HIGH = lax.Precision.HIGHEST
F32 = jnp.float32
BF16 = jnp.bfloat16
PAD = 8


def nn(a, b, precision=None):
    return lax.dot_general(a, b, (((1,), (0,)), ((), ())), precision=precision, preferred_element_type=F32)


def nt(a, b, precision=None):
    return lax.dot_general(a, b, (((1,), (1,)), ((), ())), precision=precision, preferred_element_type=F32)


def tn(a, b, precision=None):
    return lax.dot_general(a, b, (((0,), (0,)), ((), ())), precision=precision, preferred_element_type=F32)


def kernel(
    levels, head_count, total,
    q_ref, k_ref, v_ref, ld_ref, lw_ref, z_ref, gain_ref, dy_ref,
    lo_ref, gq_ref, gk_ref, gv_ref, gl_ref, gz_ref, gg_ref,
    run_s, tail_s, runc_s, tailc_s, lev_s, own_s, oth_s, w_s, sd_s, mt_s, gst_s, qst_s, qt_s,
    mixed_s, bks_s, taken_s, fac_s, acc_s, nsend_s, nrecv_s, col_s, gx_s,
    e_s, er_s, bg_s, bgr_s, dmsg_s, dr_s, d_s, dfull_s, gkin_s, gvin_s, gsend_s, grecv_s,
    a_send, a_recv, f_send, n_send, n_recv, e_send, e_recv, b_send, b_recv,
    d_send, d_recv, h_send, h_recv, g_send, g_recv,
):
    heads, width, state = q_ref.shape
    hf = width // 2
    hh = heads // 2
    depth = width.bit_length() - 1
    me = lax.axis_index("seq")
    zed = lax.axis_index("head")
    core = me % 2

    def flip(bit):
        step = 1 << bit
        return me + step - 2 * step * ((me // step) % 2)

    def upper(bit):
        return (me // (1 << bit)) % 2 == 1

    mates = [flip(bit) for bit in range(levels)]
    sibling = mates[0]
    own_start = core * hh
    other_start = hh - own_start

    def rcopy(src, dst, ssem, rsem, target):
        return pltpu.make_async_remote_copy(
            src_ref=src, dst_ref=dst, send_sem=ssem, recv_sem=rsem,
            device_id=target, device_id_type=pl.DeviceIdType.MESH,
        )

    def state_copy(start, half):
        part = pl.ds(start, hh)
        return rcopy(own_s.at[0, part], oth_s.at[0, part], a_send.at[0, half], a_recv.at[0, half], {"seq": sibling})

    def link_copy(bit, i, target):
        h = own_start + i
        return rcopy(own_s.at[bit, h], oth_s.at[bit, h], a_send.at[bit, h], a_recv.at[bit, h], {"seq": target})

    def pass_copy(bit, h):
        return rcopy(oth_s.at[bit, h], oth_s.at[bit, h], f_send.at[bit, h], a_recv.at[bit, h], {"seq": sibling})

    def norm_copy(d):
        peer = lax.rem(zed + d, head_count)
        return rcopy(nsend_s, nrecv_s.at[d - 1], n_send.at[d - 1], n_recv.at[d - 1], {"head": peer})

    def e_copy():
        return rcopy(e_s.at[pl.ds(other_start, hh)], er_s, e_send, e_recv, {"seq": sibling})

    def bg_copy():
        return rcopy(bg_s, bgr_s, b_send, b_recv, {"seq": sibling})

    def d_copy(bit, i, target):
        return rcopy(dmsg_s.at[bit, i], dr_s.at[bit, i], d_send.at[bit, i], d_recv.at[bit, i], {"seq": target})

    def half_copy(h):
        return rcopy(dfull_s.at[h], dfull_s.at[h], h_send.at[h], h_recv.at[h], {"seq": sibling})

    def gain_copy(bit):
        return rcopy(gsend_s.at[bit], grecv_s.at[bit], g_send.at[bit], g_recv.at[bit], {"seq": mates[bit]})

    barrier = pltpu.get_barrier_semaphore()
    for mate in mates:
        pl.semaphore_signal(barrier, inc=1, device_id={"seq": mate}, device_id_type=pl.DeviceIdType.MESH)
    for d in range(1, head_count):
        peer = lax.rem(zed + d, head_count)
        pl.semaphore_signal(barrier, inc=1, device_id={"head": peer}, device_id_type=pl.DeviceIdType.MESH)

    low = lax.broadcasted_iota(jnp.int32, (width, width), 0)
    high = lax.broadcasted_iota(jnp.int32, (width, width), 1)
    running = nn(ld_ref[...], jnp.where(low <= high, 1.0, 0.0), HIGH)
    ending = jnp.broadcast_to(running[:, width - 1 : width], (heads, width))
    tail = jnp.exp(ending - running)
    running_c = running.T
    tail_c = tail.T
    for h in range(heads):
        run_s[h] = running[h : h + 1]
        tail_s[h] = tail[h : h + 1]
        runc_s[h] = jnp.broadcast_to(running_c[:, h : h + 1], (width, hf))
        tailc_s[h] = jnp.broadcast_to(tail_c[:, h : h + 1], (width, hf))
        own_s[0, h, state:] = jnp.broadcast_to(ending[h : h + 1, :hf], (PAD, hf))

    row = lax.broadcasted_iota(jnp.int32, (hf, hf), 0)
    column = lax.broadcasted_iota(jnp.int32, (hf, hf), 1)
    crossed = jnp.bitwise_xor(row, column)
    level = jnp.zeros((hf, hf), jnp.int32)
    for shift in range(depth - 1):
        level = level + jnp.where(crossed >= (1 << shift), 1, 0)
    lev_s[...] = jnp.where(row <= column, level, -1)
    gst_s[hf:, :hf] = jnp.zeros((hf, hf), BF16)
    acc_s[...] = jnp.zeros_like(acc_s)

    def own_state(h):
        scaled = (k_ref[h].astype(F32) * tailc_s[h]).astype(BF16)
        own_s[0, h, :state] = tn(scaled, v_ref[h])

    @pl.loop(0, hh)
    def _(i):
        own_state(other_start + i)

    pl.semaphore_wait(barrier, levels + head_count - 1)
    state_copy(other_start, 0).start()

    @pl.loop(0, hh)
    def _(i):
        own_state(own_start + i)

    state_copy(own_start, 1).start()

    def forward(h):
        q, k, v = q_ref[h], k_ref[h], v_ref[h]
        run, runc, lw = run_s[h], runc_s[h], lw_ref[h]
        lev = lev_s[...]
        top = nt(k[:hf], q)
        low_scores = nt(k[hf:], q[hf:])

        def diagonal(place, scores, lo):
            spread = jnp.where(lev >= 0, run[:, lo : lo + hf] - runc[lo : lo + hf], 0.0)
            decay = jnp.exp(spread)
            chosen = jnp.where(lev == 0, lw[0:1, lo : lo + hf], 0.0)
            for step in range(1, depth):
                chosen = jnp.where(lev == step, lw[step : step + 1, lo : lo + hf], chosen)
            weight = decay * chosen
            w_s[h, place] = weight
            sd_s[h, place] = scores * decay
            mt_s[h, lo : lo + hf, lo : lo + hf] = (scores * weight).astype(BF16)

        diagonal(0, top[:, :hf], 0)
        diagonal(2, low_scores, hf)
        decay = jnp.exp(run[:, hf:] - runc[:hf])
        weight = decay * lw[depth : depth + 1, hf:]
        scores = top[:, hf:]
        w_s[h, 1] = weight
        sd_s[h, 1] = scores * decay
        mt_s[h, :hf, hf:] = (scores * weight).astype(BF16)
        mt_s[h, hf:, :hf] = jnp.zeros((hf, hf), BF16)
        mixed_s[h] = tn(mt_s[h], v)
        qt = q.astype(F32).T
        qt_s[h] = qt
        reach = lw[depth + 1 : depth + 1 + levels] * jnp.exp(run)
        for bit in range(levels):
            qst_s[h, bit * state : (bit + 1) * state] = (qt * reach[bit : bit + 1]).astype(BF16)

    def merge(bit, i):
        h = own_start + i
        mine, theirs = own_s[bit, h], oth_s[bit, h]
        own_rate, other_rate = mine[state : state + 1], theirs[state : state + 1]
        own_f = jnp.where(upper(bit), 1.0, jnp.exp(other_rate))
        other_f = jnp.where(upper(bit), jnp.exp(own_rate), 1.0)
        own_s[bit + 1, h, :state] = own_f * mine[:state] + other_f * theirs[:state]
        own_s[bit + 1, h, state:] = mine[state:] + theirs[state:]

    lead = min(2, heads)

    @pl.loop(0, lead)
    def _(h):
        forward(h)

    state_copy(own_start, 0).wait_recv()
    state_copy(own_start, 1).wait_recv()
    if levels > 1:

        @pl.loop(0, hh)
        def _(i):
            merge(0, i)
            link_copy(1, i, mates[1]).start()

    done = lead
    for bit in range(1, levels - 1):
        upto = min(heads, done + 2)

        @pl.loop(done, upto)
        def _(h):
            forward(h)

        done = upto
        ahead_of = min(heads - done, hh)

        @pl.loop(0, hh)
        def _(i, bit=bit, done=done, ahead_of=ahead_of):
            link_copy(bit, i, mates[bit]).wait_recv()
            merge(bit, i)
            link_copy(bit + 1, i, mates[bit + 1]).start()
            pass_copy(bit, own_start + i).start()

            @pl.when(i < ahead_of)
            def _():
                forward(done + i)

        done += ahead_of

    if done < heads:

        @pl.loop(done, heads)
        def _(h):
            forward(h)

    def outer(h):
        ahead = jnp.zeros((1, state), F32)
        for bit in range(levels):
            taken = jnp.where(upper(bit), jnp.exp(ahead), 0.0)
            taken_s[bit, h] = taken
            bks_s[h, bit * state : (bit + 1) * state] = (taken * oth_s[bit, h, :state]).astype(BF16)
            ahead = ahead + jnp.where(upper(bit), oth_s[bit, h, state : state + 1], 0.0)
        mixed = mixed_s[h] + tn(qst_s[h], bks_s[h])
        mixed_s[h] = mixed
        z = z_ref[h].astype(F32)
        gated = mixed * (z * jax.nn.sigmoid(z))
        scaled = dy_ref[h].astype(F32) * gain_ref[pl.ds(h, 1), :]
        acc_s[0] += gated * gated
        acc_s[1] += gated * scaled

    @pl.loop(0, hh)
    def _(i):
        h = own_start + i
        if levels > 1:
            link_copy(levels - 1, i, mates[levels - 1]).wait_recv()
            pass_copy(levels - 1, h).start()
        outer(h)

    @pl.loop(0, hh)
    def _(i):
        h = other_start + i
        for bit in range(1, levels):
            pass_copy(bit, h).wait_recv()
        outer(h)

    pick = lax.broadcasted_iota(jnp.int32, (8, state), 0)
    sums = nt(jnp.where(pick == 0, 1.0, 0.0), acc_s[0], HIGH) + nt(jnp.where(pick == 1, 1.0, 0.0), acc_s[1], HIGH)
    nsend_s[...] = sums
    for d in range(1, head_count):
        norm_copy(d).start()
    for d in range(1, head_count):
        norm_copy(d).wait_recv()
        sums = sums + nrecv_s[d - 1]
    inverse = lax.rsqrt(sums[0:1] / total + EPSILON)
    pull = inverse * inverse * inverse * sums[1:2] / total
    columns = jnp.where(lax.broadcasted_iota(jnp.int32, (8, width), 0) == 0, inverse, pull).T
    col_s[0] = jnp.broadcast_to(columns[:, 0:1], (width, state))
    col_s[1] = jnp.broadcast_to(columns[:, 1:2], (width, state))

    def gate_back(h):
        z = z_ref[h].astype(F32)
        sig = jax.nn.sigmoid(z)
        act = z * sig
        mixed = mixed_s[h]
        gated = mixed * act
        gain = gain_ref[pl.ds(h, 1), :]
        dy = dy_ref[h].astype(F32)
        inv = col_s[0]
        normed = gated * inv
        lo_ref[h] = (gain * normed).astype(BF16)
        gsend_s[0, pl.ds(h, 1), :] = jnp.sum(dy * normed, axis=0, keepdims=True)
        grad = inv * (dy * gain) - gated * col_s[1]
        gz_ref[h] = (grad * mixed * sig * (1.0 + z * (1.0 - sig))).astype(BF16)
        gx = (grad * act).astype(BF16)
        gx_s[h] = gx
        grads = nn(qst_s[h], gx)
        bg_s[h] = taken_s[0, h] * grads[:state]
        for bit in range(1, levels):
            e_s[h, bit - 1] = taken_s[bit, h] * grads[bit * state : (bit + 1) * state]

    @pl.loop(0, hh)
    def _(i):
        gate_back(other_start + i)

    if levels > 1:
        e_copy().start()

    @pl.loop(0, hh)
    def _(i):
        gate_back(own_start + i)

    bg_copy().start()
    gain_copy(0).start()

    def send_down(bit, i):
        h = own_start + i
        e = e_s[h, bit - 1] + er_s[i, bit - 1]
        if bit < levels - 1:
            rate, other_rate = own_s[bit, h, state : state + 1], oth_s[bit, h, state : state + 1]
            other_f = jnp.where(upper(bit), jnp.exp(rate), 1.0)
            e = e + other_f * d_s[i]
        dmsg_s[bit, i] = e
        d_copy(bit, i, mates[bit]).start()

    def take_down(bit, i):
        h = own_start + i
        d_copy(bit, i, mates[bit]).wait_recv()
        got = dr_s[bit, i]
        if bit < levels - 1:
            other_rate = oth_s[bit, h, state : state + 1]
            own_f = jnp.where(upper(bit), 1.0, jnp.exp(other_rate))
            got = got + own_f * d_s[i]
        if bit > 1:
            d_s[i] = got
        else:
            dfull_s[h] = got

    if levels > 1:
        e_copy().wait_recv()

        @pl.loop(0, hh)
        def _(i):
            send_down(levels - 1, i)
    else:
        dfull_s[...] = jnp.zeros_like(dfull_s)

    def block_grads(h):
        q, k, v, gx = q_ref[h], k_ref[h], v_ref[h], gx_s[h]
        lev = lev_s[...]
        top = nt(v[:hf], gx)
        low_grads = nt(v[hf:], gx[hf:])
        for place, part, lo in ((0, top[:, :hf], 0), (2, low_grads, hf)):
            gst_s[lo : lo + hf, lo : lo + hf] = (part * w_s[h, place]).astype(BF16)
            moved = part * sd_s[h, place]
            for step in range(depth):
                gl_ref[h, step : step + 1, lo : lo + hf] = jnp.sum(
                    jnp.where(lev == step, moved, 0.0), axis=0, keepdims=True
                )
        part = top[:, hf:]
        gst_s[:hf, hf:] = (part * w_s[h, 1]).astype(BF16)
        gl_ref[h, depth : depth + 1, :hf] = jnp.zeros((1, hf), F32)
        gl_ref[h, depth : depth + 1, hf:] = jnp.sum(part * sd_s[h, 1], axis=0, keepdims=True)
        gst = gst_s[...]
        gkin_s[h] = nn(gst, q)
        gvin_s[h] = nn(mt_s[h], gx)
        gqt = tn(k, gst)
        pulled = nt(bks_s[h], gx)
        exp_run = jnp.exp(run_s[h])
        qt = qt_s[h]
        for bit in range(levels):
            here = pulled[bit * state : (bit + 1) * state]
            at = depth + 1 + bit
            gl_ref[h, at : at + 1, :] = exp_run * jnp.sum(qt * here, axis=0, keepdims=True)
            gqt = gqt + (lw_ref[h, at : at + 1, :] * exp_run) * here
        rest = depth + 1 + levels
        gl_ref[h, rest:, :] = jnp.zeros((lw_ref.shape[1] - rest, width), F32)
        gq_ref[h] = gqt.T.astype(BF16)

    done = 0
    for bit in range(levels - 1, 0, -1):
        upto = min(heads, done + 2)

        @pl.loop(done, upto)
        def _(h):
            block_grads(h)

        done = upto
        ahead_of = min(heads - done, hh)
        turn = levels - 1 - bit
        gain_copy(turn).wait_recv()
        gsend_s[turn + 1] = gsend_s[turn] + grecv_s[turn]
        gain_copy(turn + 1).start()

        @pl.loop(0, hh)
        def _(i, bit=bit, done=done, ahead_of=ahead_of):
            take_down(bit, i)
            if bit > 1:
                send_down(bit - 1, i)
            else:
                half_copy(own_start + i).start()

            @pl.when(i < ahead_of)
            def _():
                block_grads(done + i)

        done += ahead_of

    if done < heads:

        @pl.loop(done, heads)
        def _(h):
            block_grads(h)

    gain_copy(levels - 1).wait_recv()
    gg_ref[...] = gsend_s[levels - 1] + grecv_s[levels - 1]
    bg_copy().wait_recv()

    def finish(h):
        own_f = jnp.where(upper(0), 1.0, jnp.exp(oth_s[0, h, state : state + 1]))
        down = (own_f * dfull_s[h] + bgr_s[h]).astype(BF16)
        tail = tailc_s[h]
        gk_ref[h] = (gkin_s[h] + tail * nt(v_ref[h], down)).astype(BF16)
        gv_ref[h] = (gvin_s[h] + tail * nn(k_ref[h], down)).astype(BF16)

    @pl.loop(0, hh)
    def _(i):
        finish(own_start + i)

    @pl.loop(0, hh)
    def _(i):
        h = other_start + i
        if levels > 1:
            half_copy(h).wait_recv()
        finish(h)

    state_copy(other_start, 0).wait_send()
    state_copy(own_start, 1).wait_send()
    bg_copy().wait_send()
    for d in range(1, head_count):
        norm_copy(d).wait_send()
    for bit in range(levels):
        gain_copy(bit).wait_send()
    if levels > 1:
        e_copy().wait_send()

        @pl.loop(0, hh)
        def _(i):
            half_copy(own_start + i).wait_send()
            for bit in range(1, levels):
                link_copy(bit, i, mates[bit]).wait_send()
                pass_copy(bit, own_start + i).wait_send()
                d_copy(bit, i, mates[bit]).wait_send()


def local(levels, head_count, queries, keys, values, log_decay, level_weight, gate_input, norm_gain, out_grad):
    heads, width, state = queries.shape
    feature = values.shape[2]
    hf, hh = width // 2, heads // 2
    total = heads * head_count * feature
    tokens = jax.ShapeDtypeStruct(queries.shape, BF16)
    vmem = pl.BlockSpec(memory_space=pltpu.VMEM)

    def f32(*shape):
        return pltpu.VMEM(shape, F32)

    def bf16(*shape):
        return pltpu.VMEM(shape, BF16)

    dma = pltpu.SemaphoreType.DMA
    more = max(levels - 1, 1)
    scratch = [
        f32(heads, 1, width), f32(heads, 1, width), f32(heads, width, hf), f32(heads, width, hf),
        pltpu.VMEM((hf, hf), jnp.int32),
        f32(levels, heads, state + PAD, feature), f32(levels, heads, state + PAD, feature),
        f32(heads, 3, hf, hf), f32(heads, 3, hf, hf), bf16(heads, width, width), bf16(width, width),
        bf16(heads, levels * state, width), f32(heads, state, width),
        f32(heads, width, feature), bf16(heads, levels * state, feature), f32(levels, heads, 1, feature),
        f32(8, 128), f32(2, width, feature), f32(8, width), f32(max(head_count - 1, 1), 8, width),
        f32(2, width, feature), bf16(heads, width, feature),
        f32(heads, more, state, feature), f32(hh, more, state, feature),
        f32(heads, state, feature), f32(heads, state, feature),
        f32(levels, hh, state, feature), f32(levels, hh, state, feature), f32(hh, state, feature),
        f32(heads, state, feature), f32(heads, width, state), f32(heads, width, feature),
        f32(levels, heads, feature), f32(levels, heads, feature),
        dma((levels, heads)), dma((levels, heads)), dma((levels, heads)),
        dma((max(head_count - 1, 1),)), dma((max(head_count - 1, 1),)), dma, dma, dma, dma,
        dma((levels, hh)), dma((levels, hh)), dma((heads,)), dma((heads,)), dma((levels,)), dma((levels,)),
    ]
    return pl.pallas_call(
        functools.partial(kernel, levels, head_count, total),
        out_shape=(
            tokens, tokens, tokens, tokens,
            jax.ShapeDtypeStruct(level_weight.shape, F32), tokens,
            jax.ShapeDtypeStruct(norm_gain.shape, F32),
        ),
        in_specs=[vmem] * 8,
        out_specs=(vmem,) * 7,
        scratch_shapes=scratch,
        compiler_params=pltpu.CompilerParams(
            collective_id=0, has_side_effects=True, vmem_limit_bytes=48 * 1024 * 1024
        ),
    )(queries, keys, values, log_decay, level_weight, gate_input, norm_gain, out_grad)


def solution(mesh):
    levels = mesh.shape["seq"].bit_length() - 1
    tokens = P("head", "seq", None)
    in_specs = (tokens, tokens, tokens, P("head", "seq"), P("head", None, "seq"), tokens, P("head", None), tokens)
    out_specs = (tokens, tokens, tokens, tokens, P("head", None, "seq"), tokens, P("head", None))
    return jax.shard_map(
        functools.partial(local, levels, mesh.shape["head"]),
        mesh=mesh, in_specs=in_specs, out_specs=out_specs, check_vma=False,
    )
```

```python
import functools

import jax
import jax.numpy as jnp
from jax import lax
from jax.experimental import pallas as pl
from jax.experimental.pallas import tpu as pltpu
from jax.sharding import PartitionSpec as P

EPSILON = 1e-05
HIGH = lax.Precision.HIGHEST
F32 = jnp.float32
BF16 = jnp.bfloat16
PAD = 8


def nn(a, b, precision=None):
    return lax.dot_general(a, b, (((1,), (0,)), ((), ())), precision=precision, preferred_element_type=F32)


def nt(a, b, precision=None):
    return lax.dot_general(a, b, (((1,), (1,)), ((), ())), precision=precision, preferred_element_type=F32)


def tn(a, b, precision=None):
    return lax.dot_general(a, b, (((0,), (0,)), ((), ())), precision=precision, preferred_element_type=F32)


def kernel(
    levels, head_count, total,
    q_in, k_in, v_in, ld_in, lw_in, z_in, gain_in, dy_in,
    lo_ref, gq_ref, gk_ref, gv_ref, gl_ref, gz_ref, gg_ref,
    k_ref, v_ref, gkin_s, gvin_s, tailc_s, q_ref, ld_ref, lw_ref, z_ref, gain_ref, dy_ref,
    run_s, tail_s, runc_s, lev_s, own_s, oth_s, w_s, sd_s, mt_s, qst_s, qt_s,
    mixed_s, bks_s, taken_s, acc_s, nsend_s, nrecv_s, col_s, gx_s,
    e_s, er_s, bg_s, bgr_s, dmsg_s, dr_s, d_s, dfull_s, gsend_s, grecv_s,
    in_sem,
    a_send, a_recv, f_send, n_send, n_recv, e_send, e_recv, b_send, b_recv,
    d_send, d_recv, h_send, h_recv, g_send, g_recv,
):
    heads, width, state = q_ref.shape
    hf = width // 2
    hh = heads // 2
    depth = width.bit_length() - 1
    me = lax.axis_index("seq")
    zed = lax.axis_index("head")
    core = me % 2

    def flip(bit):
        step = 1 << bit
        return me + step - 2 * step * ((me // step) % 2)

    def upper(bit):
        return (me // (1 << bit)) % 2 == 1

    mates = [flip(bit) for bit in range(levels)]
    sibling = mates[0]
    own_start = core * hh
    other_start = hh - own_start

    def rcopy(src, dst, ssem, rsem, target):
        return pltpu.make_async_remote_copy(
            src_ref=src, dst_ref=dst, send_sem=ssem, recv_sem=rsem,
            device_id=target, device_id_type=pl.DeviceIdType.MESH,
        )

    def state_copy(start, half):
        part = pl.ds(start, hh)
        return rcopy(own_s.at[0, part], oth_s.at[0, part], a_send.at[0, half], a_recv.at[0, half], {"seq": sibling})

    def link_copy(bit, i, target):
        h = own_start + i
        return rcopy(own_s.at[bit, h], oth_s.at[bit, h], a_send.at[bit, h], a_recv.at[bit, h], {"seq": target})

    def pass_copy(bit, h):
        return rcopy(oth_s.at[bit, h], oth_s.at[bit, h], f_send.at[bit, h], a_recv.at[bit, h], {"seq": sibling})

    def norm_copy(d):
        peer = lax.rem(zed + d, head_count)
        return rcopy(nsend_s, nrecv_s.at[d - 1], n_send.at[d - 1], n_recv.at[d - 1], {"head": peer})

    def e_copy():
        return rcopy(e_s.at[pl.ds(other_start, hh)], er_s, e_send, e_recv, {"seq": sibling})

    def bg_copy():
        return rcopy(bg_s, bgr_s, b_send, b_recv, {"seq": sibling})

    def d_copy(bit, i, target):
        return rcopy(dmsg_s.at[bit, i], dr_s.at[bit, i], d_send.at[bit, i], d_recv.at[bit, i], {"seq": target})

    def half_copy(h):
        return rcopy(dfull_s.at[h], dfull_s.at[h], h_send.at[h], h_recv.at[h], {"seq": sibling})

    def gain_copy(bit):
        return rcopy(gsend_s.at[bit], grecv_s.at[bit], g_send.at[bit], g_recv.at[bit], {"seq": mates[bit]})

    loads = [
        pltpu.make_async_copy(src, dst, in_sem.at[at])
        for at, (src, dst) in enumerate(
            [(ld_in, ld_ref), (k_in, k_ref), (v_in, v_ref), (q_in, q_ref), (lw_in, lw_ref),
             (z_in, z_ref), (dy_in, dy_ref), (gain_in, gain_ref)]
        )
    ]
    for load in loads:
        load.start()
    group = 2 if hh % 2 == 0 else 1

    def together(work, places):
        for store in [work(place) for place in places]:
            store()

    def sweep(work, start, count):
        @pl.loop(0, count // group)
        def _(i):
            together(work, [start + group * i + n for n in range(group)])

    barrier = pltpu.get_barrier_semaphore()
    for mate in mates:
        pl.semaphore_signal(barrier, inc=1, device_id={"seq": mate}, device_id_type=pl.DeviceIdType.MESH)
    for d in range(1, head_count):
        peer = lax.rem(zed + d, head_count)
        pl.semaphore_signal(barrier, inc=1, device_id={"head": peer}, device_id_type=pl.DeviceIdType.MESH)

    loads[0].wait()

    low = lax.broadcasted_iota(jnp.int32, (width, width), 0)
    high = lax.broadcasted_iota(jnp.int32, (width, width), 1)
    running = nn(ld_ref[...], jnp.where(low <= high, 1.0, 0.0), HIGH)
    ending = jnp.broadcast_to(running[:, width - 1 : width], (heads, width))
    tail = jnp.exp(ending - running)
    running_c = running.T
    tail_c = tail.T
    for h in range(heads):
        run_s[h] = running[h : h + 1]
        tail_s[h] = tail[h : h + 1]
        runc_s[h] = jnp.broadcast_to(running_c[:, h : h + 1], (width, hf))
        tailc_s[h] = jnp.broadcast_to(tail_c[:, h : h + 1], (width, hf))
        own_s[0, h, state:] = jnp.broadcast_to(ending[h : h + 1, :hf], (PAD, hf))

    row = lax.broadcasted_iota(jnp.int32, (hf, hf), 0)
    column = lax.broadcasted_iota(jnp.int32, (hf, hf), 1)
    crossed = jnp.bitwise_xor(row, column)
    level = jnp.zeros((hf, hf), jnp.int32)
    for shift in range(depth - 1):
        level = level + jnp.where(crossed >= (1 << shift), 1, 0)
    lev_s[...] = jnp.where(row <= column, level, -1)
    acc_s[...] = jnp.zeros_like(acc_s)

    def own_state(h):
        scaled = (k_ref[h].astype(F32) * tailc_s[h]).astype(BF16)
        summed = tn(scaled, v_ref[h])

        def store():
            own_s[0, h, :state] = summed

        return store

    loads[1].wait()
    loads[2].wait()
    sweep(own_state, other_start, hh)
    pl.semaphore_wait(barrier, levels + head_count - 1)
    state_copy(other_start, 0).start()

    sweep(own_state, own_start, hh)
    state_copy(own_start, 1).start()
    loads[3].wait()
    loads[4].wait()

    def forward(h):
        q, k, v = q_ref[h], k_ref[h], v_ref[h]
        run, runc = run_s[h], runc_s[h]
        lw = [lw_ref[step, pl.ds(h, 1), :] for step in range(depth + 1 + levels)]
        lev = lev_s[...]
        top = nt(k[:hf], q)
        low_scores = nt(k[hf:], q[hf:])

        def diagonal(scores, lo):
            spread = jnp.where(lev >= 0, run[:, lo : lo + hf] - runc[lo : lo + hf], 0.0)
            decay = jnp.exp(spread)
            chosen = jnp.where(lev == 0, lw[0][:, lo : lo + hf], 0.0)
            for step in range(1, depth):
                chosen = jnp.where(lev == step, lw[step][:, lo : lo + hf], chosen)
            weight = decay * chosen
            return weight, scores * decay, (scores * weight).astype(BF16)

        first = diagonal(top[:, :hf], 0)
        last = diagonal(low_scores, hf)
        decay = jnp.exp(run[:, hf:] - runc[:hf])
        weight = decay * lw[depth][:, hf:]
        scores = top[:, hf:]
        corner = weight, scores * decay, (scores * weight).astype(BF16)
        mt = jnp.concatenate(
            [
                jnp.concatenate([first[2], corner[2]], axis=1),
                jnp.concatenate([jnp.zeros((hf, hf), BF16), last[2]], axis=1),
            ],
            axis=0,
        )
        mixed = tn(mt, v)
        qt = q.astype(F32).T
        exp_run = jnp.exp(run)
        scaled = [(qt * (lw[depth + 1 + bit] * exp_run)).astype(BF16) for bit in range(levels)]

        def store():
            for place, part in enumerate((first, corner, last)):
                w_s[h, place] = part[0]
                sd_s[h, place] = part[1]
            mt_s[h] = mt
            mixed_s[h] = mixed
            qt_s[h] = qt
            for bit in range(levels):
                qst_s[h, bit * state : (bit + 1) * state] = scaled[bit]

        return store

    def merge(bit, i):
        h = own_start + i
        mine, theirs = own_s[bit, h], oth_s[bit, h]
        own_rate, other_rate = mine[state : state + 1], theirs[state : state + 1]
        own_f = jnp.where(upper(bit), 1.0, jnp.exp(other_rate))
        other_f = jnp.where(upper(bit), jnp.exp(own_rate), 1.0)
        own_s[bit + 1, h, :state] = own_f * mine[:state] + other_f * theirs[:state]
        own_s[bit + 1, h, state:] = mine[state:] + theirs[state:]

    together(forward, range(group))
    done = group
    state_copy(own_start, 0).wait_recv()
    state_copy(own_start, 1).wait_recv()
    if levels > 1:

        @pl.loop(0, hh)
        def _(i):
            merge(0, i)
            link_copy(1, i, mates[1]).start()

    for bit in range(1, levels - 1):
        if done + group <= heads:
            together(forward, range(done, done + group))
            done += group
        ahead_of = min(heads - done, hh)

        @pl.loop(0, hh // group)
        def _(j, bit=bit, done=done, ahead_of=ahead_of):
            for n in range(group):
                i = group * j + n
                link_copy(bit, i, mates[bit]).wait_recv()
                merge(bit, i)
                link_copy(bit + 1, i, mates[bit + 1]).start()
                pass_copy(bit, own_start + i).start()

            @pl.when(group * j < ahead_of)
            def _():
                together(forward, [done + group * j + n for n in range(group)])

        done += ahead_of

    if done < heads:
        sweep(forward, done, heads - done)

    def outer(h):
        ahead = jnp.zeros((1, state), F32)
        shares, buckets = [], []
        for bit in range(levels):
            taken = jnp.where(upper(bit), jnp.exp(ahead), 0.0)
            shares.append(taken)
            buckets.append((taken * oth_s[bit, h, :state]).astype(BF16))
            ahead = ahead + jnp.where(upper(bit), oth_s[bit, h, state : state + 1], 0.0)
        mixed = mixed_s[h] + tn(qst_s[h], jnp.concatenate(buckets, axis=0))
        z = z_ref[h].astype(F32)
        gated = mixed * (z * jax.nn.sigmoid(z))
        scaled = dy_ref[h].astype(F32) * gain_ref[pl.ds(h, 1), :]

        def store():
            for bit in range(levels):
                taken_s[bit, h] = shares[bit]
                bks_s[h, bit * state : (bit + 1) * state] = buckets[bit]
            mixed_s[h] = mixed
            acc_s[0] += gated * gated
            acc_s[1] += gated * scaled

        return store

    for load in loads[5:]:
        load.wait()

    @pl.loop(0, hh // group)
    def _(j):
        places = [own_start + group * j + n for n in range(group)]
        if levels > 1:
            for n in range(group):
                link_copy(levels - 1, group * j + n, mates[levels - 1]).wait_recv()
                pass_copy(levels - 1, places[n]).start()
        together(outer, places)

    @pl.loop(0, hh // group)
    def _(j):
        places = [other_start + group * j + n for n in range(group)]
        for h in places:
            for bit in range(1, levels):
                pass_copy(bit, h).wait_recv()
        together(outer, places)

    pick = lax.broadcasted_iota(jnp.int32, (8, state), 0)
    sums = nt(jnp.where(pick == 0, 1.0, 0.0), acc_s[0], HIGH) + nt(jnp.where(pick == 1, 1.0, 0.0), acc_s[1], HIGH)
    nsend_s[...] = sums
    for d in range(1, head_count):
        norm_copy(d).start()
    for d in range(1, head_count):
        norm_copy(d).wait_recv()
        sums = sums + nrecv_s[d - 1]
    inverse = lax.rsqrt(sums[0:1] / total + EPSILON)
    pull = inverse * inverse * inverse * sums[1:2] / total
    columns = jnp.where(lax.broadcasted_iota(jnp.int32, (8, width), 0) == 0, inverse, pull).T
    col_s[0] = jnp.broadcast_to(columns[:, 0:1], (width, state))
    col_s[1] = jnp.broadcast_to(columns[:, 1:2], (width, state))

    def gate_back(h):
        z = z_ref[h].astype(F32)
        sig = jax.nn.sigmoid(z)
        act = z * sig
        mixed = mixed_s[h]
        gated = mixed * act
        gain = gain_ref[pl.ds(h, 1), :]
        dy = dy_ref[h].astype(F32)
        inv = col_s[0]
        normed = gated * inv
        shown = (gain * normed).astype(BF16)
        gain_sum = jnp.sum(dy * normed, axis=0, keepdims=True)
        grad = inv * (dy * gain) - gated * col_s[1]
        gz = (grad * mixed * sig * (1.0 + z * (1.0 - sig))).astype(BF16)
        gx = (grad * act).astype(BF16)
        grads = nn(qst_s[h], gx)
        parts = [taken_s[bit, h] * grads[bit * state : (bit + 1) * state] for bit in range(levels)]

        def store():
            lo_ref[h] = shown
            gsend_s[0, pl.ds(h, 1), :] = gain_sum
            gz_ref[h] = gz
            gx_s[h] = gx
            bg_s[h] = parts[0]
            for bit in range(1, levels):
                e_s[h, bit - 1] = parts[bit]

        return store

    sweep(gate_back, other_start, hh)
    if levels > 1:
        e_copy().start()

    sweep(gate_back, own_start, hh)
    bg_copy().start()
    gain_copy(0).start()

    def send_down(bit, i):
        h = own_start + i
        e = e_s[h, bit - 1] + er_s[i, bit - 1]
        if bit < levels - 1:
            rate, other_rate = own_s[bit, h, state : state + 1], oth_s[bit, h, state : state + 1]
            other_f = jnp.where(upper(bit), jnp.exp(rate), 1.0)
            e = e + other_f * d_s[i]
        dmsg_s[bit, i] = e
        d_copy(bit, i, mates[bit]).start()

    def take_down(bit, i):
        h = own_start + i
        d_copy(bit, i, mates[bit]).wait_recv()
        got = dr_s[bit, i]
        if bit < levels - 1:
            other_rate = oth_s[bit, h, state : state + 1]
            own_f = jnp.where(upper(bit), 1.0, jnp.exp(other_rate))
            got = got + own_f * d_s[i]
        if bit > 1:
            d_s[i] = got
        else:
            dfull_s[h] = got

    if levels > 1:
        e_copy().wait_recv()

        @pl.loop(0, hh)
        def _(i):
            send_down(levels - 1, i)
    else:
        dfull_s[...] = jnp.zeros_like(dfull_s)

    def block_grads(h):
        q, k, v, gx = q_ref[h], k_ref[h], v_ref[h], gx_s[h]
        lev = lev_s[...]
        top = nt(v[:hf], gx)
        low_grads = nt(v[hf:], gx[hf:])
        parts = ((top[:, :hf], 0), (top[:, hf:], hf), (low_grads, hf))
        spread = [(part * w_s[h, place]).astype(BF16) for place, (part, lo) in enumerate(parts)]
        gst = jnp.concatenate(
            [
                jnp.concatenate([spread[0], spread[1]], axis=1),
                jnp.concatenate([jnp.zeros((hf, hf), BF16), spread[2]], axis=1),
            ],
            axis=0,
        )
        moved = [parts[place][0] * sd_s[h, place] for place in (0, 2)]
        rows = [
            jnp.concatenate(
                [jnp.sum(jnp.where(lev == step, part, 0.0), axis=0, keepdims=True) for part in moved], axis=1
            )
            for step in range(depth)
        ]
        corner = jnp.sum(top[:, hf:] * sd_s[h, 1], axis=0, keepdims=True)
        rows.append(jnp.concatenate([jnp.zeros((1, hf), F32), corner], axis=1))
        gkin = nn(gst, q)
        gvin = nn(mt_s[h], gx)
        gqt = tn(k, gst)
        pulled = nt(bks_s[h], gx)
        exp_run = jnp.exp(run_s[h])
        qt = qt_s[h]
        outs = []
        for bit in range(levels):
            here = pulled[bit * state : (bit + 1) * state]
            outs.append(exp_run * jnp.sum(qt * here, axis=0, keepdims=True))
            gqt = gqt + (lw_ref[depth + 1 + bit, pl.ds(h, 1), :] * exp_run) * here
        gq = gqt.T.astype(BF16)

        def store():
            here = lax.broadcasted_iota(jnp.int32, (heads, width), 0) == h
            for step, line in enumerate(rows + outs):
                gl_ref[step] = jnp.where(here, line, gl_ref[step])
            gkin_s[h] = gkin
            gvin_s[h] = gvin
            gq_ref[h] = gq

        return store

    gl_ref[...] = jnp.zeros_like(gl_ref)
    done = 0
    for bit in range(levels - 1, 0, -1):
        if done + group <= heads:
            together(block_grads, range(done, done + group))
            done += group
        ahead_of = min(heads - done, hh)
        turn = levels - 1 - bit
        gain_copy(turn).wait_recv()
        gsend_s[turn + 1] = gsend_s[turn] + grecv_s[turn]
        gain_copy(turn + 1).start()

        @pl.loop(0, hh // group)
        def _(j, bit=bit, done=done, ahead_of=ahead_of):
            for n in range(group):
                i = group * j + n
                take_down(bit, i)
                if bit > 1:
                    send_down(bit - 1, i)
                else:
                    half_copy(own_start + i).start()

            @pl.when(group * j < ahead_of)
            def _():
                together(block_grads, [done + group * j + n for n in range(group)])

        done += ahead_of

    if done < heads:
        sweep(block_grads, done, heads - done)

    gain_copy(levels - 1).wait_recv()
    gg_ref[...] = gsend_s[levels - 1] + grecv_s[levels - 1]
    bg_copy().wait_recv()

    def finish(h):
        own_f = jnp.where(upper(0), 1.0, jnp.exp(oth_s[0, h, state : state + 1]))
        down = (own_f * dfull_s[h] + bgr_s[h]).astype(BF16)
        tail = tailc_s[h]
        gk = (gkin_s[h] + tail * nt(v_ref[h], down)).astype(BF16)
        gv = (gvin_s[h] + tail * nn(k_ref[h], down)).astype(BF16)

        def store():
            gk_ref[h] = gk
            gv_ref[h] = gv

        return store

    sweep(finish, own_start, hh)
    if levels > 1:

        @pl.loop(0, hh)
        def _(i):
            half_copy(other_start + i).wait_recv()

    sweep(finish, other_start, hh)

    state_copy(other_start, 0).wait_send()
    state_copy(own_start, 1).wait_send()
    bg_copy().wait_send()
    for d in range(1, head_count):
        norm_copy(d).wait_send()
    for bit in range(levels):
        gain_copy(bit).wait_send()
    if levels > 1:
        e_copy().wait_send()

        @pl.loop(0, hh)
        def _(i):
            half_copy(own_start + i).wait_send()
            for bit in range(1, levels):
                link_copy(bit, i, mates[bit]).wait_send()
                pass_copy(bit, own_start + i).wait_send()
                d_copy(bit, i, mates[bit]).wait_send()


def copy_kernel(*refs):
    count = len(refs) // 2
    sems = refs[-1]
    copies = [pltpu.make_async_copy(refs[at], refs[count + at], sems.at[at]) for at in range(count)]
    for copy in copies:
        copy.start()
    for copy in copies:
        copy.wait()


def local(levels, head_count, queries, keys, values, log_decay, level_weight, gate_input, norm_gain, out_grad):
    heads, width, state = queries.shape
    feature = values.shape[2]
    hf, hh = width // 2, heads // 2
    total = heads * head_count * feature
    tokens = jax.ShapeDtypeStruct(queries.shape, BF16)
    vmem = pl.BlockSpec(memory_space=pltpu.VMEM)

    def f32(*shape):
        return pltpu.VMEM(shape, F32)

    def bf16(*shape):
        return pltpu.VMEM(shape, BF16)

    dma = pltpu.SemaphoreType.DMA
    more = max(levels - 1, 1)
    scratch = [
        bf16(heads, width, state), bf16(heads, width, feature),
        f32(heads, width, state), f32(heads, width, feature), f32(heads, width, feature),
        bf16(heads, width, state), f32(heads, width), f32(level_weight.shape[1], heads, width),
        bf16(heads, width, feature), f32(heads, feature), bf16(heads, width, feature),
        f32(heads, 1, width), f32(heads, 1, width), f32(heads, width, hf),
        pltpu.VMEM((hf, hf), jnp.int32),
        f32(levels, heads, state + PAD, feature), f32(levels, heads, state + PAD, feature),
        f32(heads, 3, hf, hf), f32(heads, 3, hf, hf), bf16(heads, width, width),
        bf16(heads, levels * state, width), f32(heads, state, width),
        f32(heads, width, feature), bf16(heads, levels * state, feature), f32(levels, heads, 1, feature),
        f32(2, width, feature), f32(8, width), f32(max(head_count - 1, 1), 8, width),
        f32(2, width, feature), bf16(heads, width, feature),
        f32(heads, more, state, feature), f32(hh, more, state, feature),
        f32(heads, state, feature), f32(heads, state, feature),
        f32(levels, hh, state, feature), f32(levels, hh, state, feature), f32(hh, state, feature),
        f32(heads, state, feature),
        f32(levels, heads, feature), f32(levels, heads, feature),
        dma((8,)),
        dma((levels, heads)), dma((levels, heads)), dma((levels, heads)),
        dma((max(head_count - 1, 1),)), dma((max(head_count - 1, 1),)), dma, dma, dma, dma,
        dma((levels, hh)), dma((levels, hh)), dma((heads,)), dma((heads,)), dma((levels,)), dma((levels,)),
    ]
    hbm = pl.BlockSpec(memory_space=pltpu.HBM)
    turned = jax.ShapeDtypeStruct((level_weight.shape[1], heads, width), F32)
    gains = jax.ShapeDtypeStruct(norm_gain.shape, F32)
    shapes = (tokens, tokens, tokens, tokens, turned, tokens, gains)
    outs = pl.pallas_call(
        functools.partial(kernel, levels, head_count, total),
        out_shape=shapes,
        in_specs=[hbm] * 8,
        out_specs=(vmem,) * 7,
        scratch_shapes=scratch,
        compiler_params=pltpu.CompilerParams(
            collective_id=0, has_side_effects=True, vmem_limit_bytes=51 * 1024 * 1024
        ),
    )(
        queries, keys, values, log_decay, jnp.transpose(level_weight, (1, 0, 2)), gate_input, norm_gain, out_grad
    )
    lo, gq, gk, gv, gl, gz, gg = pl.pallas_call(
        copy_kernel,
        out_shape=shapes,
        in_specs=[pl.BlockSpec(memory_space=pl.ANY)] * 7,
        out_specs=(hbm,) * 7,
        scratch_shapes=[dma((7,))],
    )(*outs)
    return lo, gq, gk, gv, jnp.transpose(gl, (1, 0, 2)), gz, gg


def solution(mesh):
    levels = mesh.shape["seq"].bit_length() - 1
    tokens = P("head", "seq", None)
    in_specs = (tokens, tokens, tokens, P("head", "seq"), P("head", None, "seq"), tokens, P("head", None), tokens)
    out_specs = (tokens, tokens, tokens, tokens, P("head", None, "seq"), tokens, P("head", None))
    return jax.shard_map(
        functools.partial(local, levels, mesh.shape["head"]),
        mesh=mesh, in_specs=in_specs, out_specs=out_specs, check_vma=False,
    )
```

```python
import functools

import jax
import jax.numpy as jnp
from jax import lax
from jax.experimental import pallas as pl
from jax.experimental.pallas import tpu as pltpu
from jax.sharding import PartitionSpec as P

EPSILON = 1e-05
HIGH = lax.Precision.HIGHEST
F32 = jnp.float32
BF16 = jnp.bfloat16
PAD = 8


def nn(a, b, precision=None):
    return lax.dot_general(a, b, (((1,), (0,)), ((), ())), precision=precision, preferred_element_type=F32)


def nt(a, b, precision=None):
    return lax.dot_general(a, b, (((1,), (1,)), ((), ())), precision=precision, preferred_element_type=F32)


def tn(a, b, precision=None):
    return lax.dot_general(a, b, (((0,), (0,)), ((), ())), precision=precision, preferred_element_type=F32)


def kernel(
    levels, head_count, total,
    q_in, k_in, v_in, ld_in, lw_in, z_in, gain_in, dy_in,
    lo_ref, gq_ref, gk_ref, gv_ref, gl_ref, gz_ref, gg_ref,
    k_ref, v_ref, gkin_s, gvin_s, tailc_s, q_ref, ld_ref, lw_ref, z_ref, gain_ref, dy_ref,
    run_s, tail_s, runc_s, lev_s, own_s, oth_s, w_s, sd_s, mt_s, qst_s, qt_s,
    mixed_s, bks_s, taken_s, acc_s, nsend_s, nrecv_s, col_s, gx_s,
    e_s, er_s, bg_s, bgr_s, dmsg_s, dr_s, d_s, dfull_s, gsend_s, grecv_s,
    in_sem,
    a_send, a_recv, f_send, n_send, n_recv, e_send, e_recv, b_send, b_recv,
    d_send, d_recv, h_send, h_recv, g_send, g_recv,
):
    heads, width, state = q_ref.shape
    hf = width // 2
    hh = heads // 2
    depth = width.bit_length() - 1
    me = lax.axis_index("seq")
    zed = lax.axis_index("head")
    core = me % 2

    def flip(bit):
        step = 1 << bit
        return me + step - 2 * step * ((me // step) % 2)

    def upper(bit):
        return (me // (1 << bit)) % 2 == 1

    mates = [flip(bit) for bit in range(levels)]
    sibling = mates[0]
    own_start = core * hh
    other_start = hh - own_start

    def rcopy(src, dst, ssem, rsem, target):
        return pltpu.make_async_remote_copy(
            src_ref=src, dst_ref=dst, send_sem=ssem, recv_sem=rsem,
            device_id=target, device_id_type=pl.DeviceIdType.MESH,
        )

    def state_copy(start, half):
        part = pl.ds(start, hh)
        return rcopy(own_s.at[0, part], oth_s.at[0, part], a_send.at[0, half], a_recv.at[0, half], {"seq": sibling})

    def link_copy(bit, i, target):
        h = own_start + i
        return rcopy(own_s.at[bit, h], oth_s.at[bit, h], a_send.at[bit, h], a_recv.at[bit, h], {"seq": target})

    def pass_copy(bit, h):
        return rcopy(oth_s.at[bit, h], oth_s.at[bit, h], f_send.at[bit, h], a_recv.at[bit, h], {"seq": sibling})

    def norm_copy(d):
        peer = lax.rem(zed + d, head_count)
        return rcopy(nsend_s, nrecv_s.at[d - 1], n_send.at[d - 1], n_recv.at[d - 1], {"head": peer})

    def e_copy():
        return rcopy(e_s.at[pl.ds(other_start, hh)], er_s, e_send, e_recv, {"seq": sibling})

    def bg_copy():
        return rcopy(bg_s, bgr_s, b_send, b_recv, {"seq": sibling})

    def d_copy(bit, i, target):
        return rcopy(dmsg_s.at[bit, i], dr_s.at[bit, i], d_send.at[bit, i], d_recv.at[bit, i], {"seq": target})

    def half_copy(h):
        return rcopy(dfull_s.at[h], dfull_s.at[h], h_send.at[h], h_recv.at[h], {"seq": sibling})

    def gain_copy(bit):
        return rcopy(gsend_s.at[bit], grecv_s.at[bit], g_send.at[bit], g_recv.at[bit], {"seq": mates[bit]})

    loads = [
        pltpu.make_async_copy(src, dst, in_sem.at[at])
        for at, (src, dst) in enumerate(
            [(ld_in, ld_ref), (k_in, k_ref), (v_in, v_ref), (q_in, q_ref), (lw_in, lw_ref),
             (z_in, z_ref), (dy_in, dy_ref), (gain_in, gain_ref)]
        )
    ]
    for load in loads:
        load.start()
    group = 2 if hh % 2 == 0 else 1

    def together(work, places):
        for store in [work(place) for place in places]:
            store()

    def sweep(work, start, count):
        @pl.loop(0, count // group)
        def _(i):
            together(work, [start + group * i + n for n in range(group)])

    barrier = pltpu.get_barrier_semaphore()
    for mate in mates:
        pl.semaphore_signal(barrier, inc=1, device_id={"seq": mate}, device_id_type=pl.DeviceIdType.MESH)
    for d in range(1, head_count):
        peer = lax.rem(zed + d, head_count)
        pl.semaphore_signal(barrier, inc=1, device_id={"head": peer}, device_id_type=pl.DeviceIdType.MESH)

    loads[0].wait()

    low = lax.broadcasted_iota(jnp.int32, (width, width), 0)
    high = lax.broadcasted_iota(jnp.int32, (width, width), 1)
    running = nn(ld_ref[...], jnp.where(low <= high, 1.0, 0.0), HIGH)
    ending = jnp.broadcast_to(running[:, width - 1 : width], (heads, width))
    tail = jnp.exp(ending - running)
    running_c = running.T
    tail_c = tail.T
    for h in range(heads):
        run_s[h] = running[h : h + 1]
        tail_s[h] = tail[h : h + 1]
        runc_s[h] = jnp.broadcast_to(running_c[:, h : h + 1], (width, hf))
        tailc_s[h] = jnp.broadcast_to(tail_c[:, h : h + 1], (width, hf))
        own_s[0, h, state:] = jnp.broadcast_to(ending[h : h + 1, :hf], (PAD, hf))

    row = lax.broadcasted_iota(jnp.int32, (hf, hf), 0)
    column = lax.broadcasted_iota(jnp.int32, (hf, hf), 1)
    crossed = jnp.bitwise_xor(row, column)
    level = jnp.zeros((hf, hf), jnp.int32)
    for shift in range(depth - 1):
        level = level + jnp.where(crossed >= (1 << shift), 1, 0)
    lev_s[...] = jnp.where(row <= column, level, -1)
    acc_s[...] = jnp.zeros_like(acc_s)

    def own_state(h):
        scaled = (k_ref[h].astype(F32) * tailc_s[h]).astype(BF16)
        summed = tn(scaled, v_ref[h])

        def store():
            own_s[0, h, :state] = summed

        return store

    loads[1].wait()
    loads[2].wait()
    sweep(own_state, other_start, hh)
    pl.semaphore_wait(barrier, levels + head_count - 1)
    state_copy(other_start, 0).start()

    sweep(own_state, own_start, hh)
    state_copy(own_start, 1).start()
    loads[3].wait()
    loads[4].wait()

    def forward(h):
        q, k, v = q_ref[h], k_ref[h], v_ref[h]
        run, runc = run_s[h], runc_s[h]
        lw = [lw_ref[step, pl.ds(h, 1), :] for step in range(depth + 1 + levels)]
        lev = lev_s[...]
        top = nt(k[:hf], q)
        low_scores = nt(k[hf:], q[hf:])

        def diagonal(scores, lo):
            spread = jnp.where(lev >= 0, run[:, lo : lo + hf] - runc[lo : lo + hf], 0.0)
            decay = jnp.exp(spread)
            chosen = jnp.where(lev == 0, lw[0][:, lo : lo + hf], 0.0)
            for step in range(1, depth):
                chosen = jnp.where(lev == step, lw[step][:, lo : lo + hf], chosen)
            weight = decay * chosen
            return weight, scores * decay, (scores * weight).astype(BF16)

        first = diagonal(top[:, :hf], 0)
        last = diagonal(low_scores, hf)
        decay = jnp.exp(run[:, hf:] - runc[:hf])
        weight = decay * lw[depth][:, hf:]
        scores = top[:, hf:]
        corner = weight, scores * decay, (scores * weight).astype(BF16)
        mt = jnp.concatenate(
            [
                jnp.concatenate([first[2], corner[2]], axis=1),
                jnp.concatenate([jnp.zeros((hf, hf), BF16), last[2]], axis=1),
            ],
            axis=0,
        )
        mixed = tn(mt, v)
        qt = q.astype(F32).T
        exp_run = jnp.exp(run)
        scaled = [(qt * (lw[depth + 1 + bit] * exp_run)).astype(BF16) for bit in range(levels)]

        def store():
            for place, part in enumerate((first, corner, last)):
                w_s[h, place] = part[0]
                sd_s[h, place] = part[1]
            mt_s[h] = mt
            mixed_s[h] = mixed
            qt_s[h] = qt
            for bit in range(levels):
                qst_s[h, bit * state : (bit + 1) * state] = scaled[bit]

        return store

    def merge(bit, i):
        h = own_start + i
        mine, theirs = own_s[bit, h], oth_s[bit, h]
        own_rate, other_rate = mine[state : state + 1], theirs[state : state + 1]
        own_f = jnp.where(upper(bit), 1.0, jnp.exp(other_rate))
        other_f = jnp.where(upper(bit), jnp.exp(own_rate), 1.0)
        own_s[bit + 1, h, :state] = own_f * mine[:state] + other_f * theirs[:state]
        own_s[bit + 1, h, state:] = mine[state:] + theirs[state:]

    together(forward, range(group))
    done = group
    state_copy(own_start, 0).wait_recv()
    state_copy(own_start, 1).wait_recv()
    if levels > 1:

        @pl.loop(0, hh)
        def _(i):
            merge(0, i)
            link_copy(1, i, mates[1]).start()

    for bit in range(1, levels - 1):
        if done + group <= heads:
            together(forward, range(done, done + group))
            done += group
        ahead_of = min(heads - done, hh)

        @pl.loop(0, hh // group)
        def _(j, bit=bit, done=done, ahead_of=ahead_of):
            for n in range(group):
                i = group * j + n
                link_copy(bit, i, mates[bit]).wait_recv()
                merge(bit, i)
                link_copy(bit + 1, i, mates[bit + 1]).start()
                pass_copy(bit, own_start + i).start()

            @pl.when(group * j < ahead_of)
            def _():
                together(forward, [done + group * j + n for n in range(group)])

        done += ahead_of

    if done < heads:
        sweep(forward, done, heads - done)

    def outer(h):
        ahead = jnp.zeros((1, state), F32)
        shares, buckets = [], []
        for bit in range(levels):
            taken = jnp.where(upper(bit), jnp.exp(ahead), 0.0)
            shares.append(taken)
            buckets.append((taken * oth_s[bit, h, :state]).astype(BF16))
            ahead = ahead + jnp.where(upper(bit), oth_s[bit, h, state : state + 1], 0.0)
        mixed = mixed_s[h] + tn(qst_s[h], jnp.concatenate(buckets, axis=0))
        z = z_ref[h].astype(F32)
        gated = mixed * (z * jax.nn.sigmoid(z))
        scaled = dy_ref[h].astype(F32) * gain_ref[pl.ds(h, 1), :]

        def store():
            for bit in range(levels):
                taken_s[bit, h] = shares[bit]
                bks_s[h, bit * state : (bit + 1) * state] = buckets[bit]
            mixed_s[h] = mixed
            acc_s[0] += gated * gated
            acc_s[1] += gated * scaled

        return store

    for load in loads[5:]:
        load.wait()

    @pl.loop(0, hh // group)
    def _(j):
        places = [own_start + group * j + n for n in range(group)]
        if levels > 1:
            for n in range(group):
                link_copy(levels - 1, group * j + n, mates[levels - 1]).wait_recv()
                pass_copy(levels - 1, places[n]).start()
        together(outer, places)

    @pl.loop(0, hh // group)
    def _(j):
        places = [other_start + group * j + n for n in range(group)]
        for h in places:
            for bit in range(1, levels):
                pass_copy(bit, h).wait_recv()
        together(outer, places)

    pick = lax.broadcasted_iota(jnp.int32, (8, state), 0)
    sums = nt(jnp.where(pick == 0, 1.0, 0.0), acc_s[0], HIGH) + nt(jnp.where(pick == 1, 1.0, 0.0), acc_s[1], HIGH)
    nsend_s[...] = sums
    for d in range(1, head_count):
        norm_copy(d).start()
    for d in range(1, head_count):
        norm_copy(d).wait_recv()
        sums = sums + nrecv_s[d - 1]
    inverse = lax.rsqrt(sums[0:1] / total + EPSILON)
    pull = inverse * inverse * inverse * sums[1:2] / total
    columns = jnp.where(lax.broadcasted_iota(jnp.int32, (8, width), 0) == 0, inverse, pull).T
    col_s[0] = jnp.broadcast_to(columns[:, 0:1], (width, state))
    col_s[1] = jnp.broadcast_to(columns[:, 1:2], (width, state))

    def gate_back(h):
        z = z_ref[h].astype(F32)
        sig = jax.nn.sigmoid(z)
        act = z * sig
        mixed = mixed_s[h]
        gated = mixed * act
        gain = gain_ref[pl.ds(h, 1), :]
        dy = dy_ref[h].astype(F32)
        inv = col_s[0]
        normed = gated * inv
        shown = (gain * normed).astype(BF16)
        gain_sum = jnp.sum(dy * normed, axis=0, keepdims=True)
        grad = inv * (dy * gain) - gated * col_s[1]
        gz = (grad * mixed * sig * (1.0 + z * (1.0 - sig))).astype(BF16)
        gx = (grad * act).astype(BF16)
        grads = nn(qst_s[h], gx)
        parts = [taken_s[bit, h] * grads[bit * state : (bit + 1) * state] for bit in range(levels)]

        def store():
            lo_ref[h] = shown
            gsend_s[0, pl.ds(h, 1), :] = gain_sum
            gz_ref[h] = gz
            gx_s[h] = gx
            bg_s[h] = parts[0]
            for bit in range(1, levels):
                e_s[h, bit - 1] = parts[bit]

        return store

    sweep(gate_back, other_start, hh)
    if levels > 1:
        e_copy().start()

    def send_down(bit, i):
        h = own_start + i
        e = e_s[h, bit - 1] + er_s[i, bit - 1]
        if bit < levels - 1:
            rate, other_rate = own_s[bit, h, state : state + 1], oth_s[bit, h, state : state + 1]
            other_f = jnp.where(upper(bit), jnp.exp(rate), 1.0)
            e = e + other_f * d_s[i]
        dmsg_s[bit, i] = e
        d_copy(bit, i, mates[bit]).start()

    def take_down(bit, i):
        h = own_start + i
        d_copy(bit, i, mates[bit]).wait_recv()
        got = dr_s[bit, i]
        if bit < levels - 1:
            other_rate = oth_s[bit, h, state : state + 1]
            own_f = jnp.where(upper(bit), 1.0, jnp.exp(other_rate))
            got = got + own_f * d_s[i]
        if bit > 1:
            d_s[i] = got
        else:
            dfull_s[h] = got

    @pl.loop(0, hh // group)
    def _(j):
        together(gate_back, [own_start + group * j + n for n in range(group)])
        if levels > 1:

            @pl.when(j == 0)
            def _():
                e_copy().wait_recv()

            for n in range(group):
                send_down(levels - 1, group * j + n)

    bg_copy().start()
    gain_copy(0).start()
    if levels == 1:
        dfull_s[...] = jnp.zeros_like(dfull_s)

    def block_grads(h):
        q, k, v, gx = q_ref[h], k_ref[h], v_ref[h], gx_s[h]
        lev = lev_s[...]
        top = nt(v[:hf], gx)
        low_grads = nt(v[hf:], gx[hf:])
        parts = ((top[:, :hf], 0), (top[:, hf:], hf), (low_grads, hf))
        spread = [(part * w_s[h, place]).astype(BF16) for place, (part, lo) in enumerate(parts)]
        gst = jnp.concatenate(
            [
                jnp.concatenate([spread[0], spread[1]], axis=1),
                jnp.concatenate([jnp.zeros((hf, hf), BF16), spread[2]], axis=1),
            ],
            axis=0,
        )
        moved = [parts[place][0] * sd_s[h, place] for place in (0, 2)]
        rows = [
            jnp.concatenate(
                [jnp.sum(jnp.where(lev == step, part, 0.0), axis=0, keepdims=True) for part in moved], axis=1
            )
            for step in range(depth)
        ]
        corner = jnp.sum(top[:, hf:] * sd_s[h, 1], axis=0, keepdims=True)
        rows.append(jnp.concatenate([jnp.zeros((1, hf), F32), corner], axis=1))
        gkin = nn(gst, q)
        gvin = nn(mt_s[h], gx)
        gqt = tn(k, gst)
        pulled = nt(bks_s[h], gx)
        exp_run = jnp.exp(run_s[h])
        qt = qt_s[h]
        outs = []
        for bit in range(levels):
            here = pulled[bit * state : (bit + 1) * state]
            outs.append(exp_run * jnp.sum(qt * here, axis=0, keepdims=True))
            gqt = gqt + (lw_ref[depth + 1 + bit, pl.ds(h, 1), :] * exp_run) * here
        gq = gqt.T.astype(BF16)

        def store():
            here = lax.broadcasted_iota(jnp.int32, (heads, width), 0) == h
            for step, line in enumerate(rows + outs):
                gl_ref[step] = jnp.where(here, line, gl_ref[step])
            gkin_s[h] = gkin
            gvin_s[h] = gvin
            gq_ref[h] = gq

        return store

    def finish(h):
        own_f = jnp.where(upper(0), 1.0, jnp.exp(oth_s[0, h, state : state + 1]))
        down = (own_f * dfull_s[h] + bgr_s[h]).astype(BF16)
        tail = tailc_s[h]
        gk = (gkin_s[h] + tail * nt(v_ref[h], down)).astype(BF16)
        gv = (gvin_s[h] + tail * nn(k_ref[h], down)).astype(BF16)

        def store():
            gk_ref[h] = gk
            gv_ref[h] = gv

        return store

    gl_ref[...] = jnp.zeros_like(gl_ref)
    done = 0
    for bit in range(levels - 1, 1, -1):
        if done + group <= heads:
            together(block_grads, range(done, done + group))
            done += group
        ahead_of = min(heads - done, hh)
        turn = levels - 1 - bit
        gain_copy(turn).wait_recv()
        gsend_s[turn + 1] = gsend_s[turn] + grecv_s[turn]
        gain_copy(turn + 1).start()

        @pl.loop(0, hh // group)
        def _(j, bit=bit, done=done, ahead_of=ahead_of):
            for n in range(group):
                i = group * j + n
                take_down(bit, i)
                send_down(bit - 1, i)

            @pl.when(group * j < ahead_of)
            def _():
                together(block_grads, [done + group * j + n for n in range(group)])

        done += ahead_of

    if done < heads:
        sweep(block_grads, done, heads - done)
    if levels > 1:
        turn = levels - 2
        gain_copy(turn).wait_recv()
        gsend_s[turn + 1] = gsend_s[turn] + grecv_s[turn]
        gain_copy(turn + 1).start()
    bg_copy().wait_recv()

    @pl.loop(0, hh // group)
    def _(j):
        places = [group * j + n for n in range(group)]
        if levels > 1:
            for i in places:
                take_down(1, i)
                half_copy(own_start + i).start()
        together(finish, [own_start + i for i in places])

    @pl.loop(0, hh // group)
    def _(j):
        places = [other_start + group * j + n for n in range(group)]
        if levels > 1:
            for h in places:
                half_copy(h).wait_recv()
        together(finish, places)

    gain_copy(levels - 1).wait_recv()
    gg_ref[...] = gsend_s[levels - 1] + grecv_s[levels - 1]
    state_copy(other_start, 0).wait_send()
    state_copy(own_start, 1).wait_send()
    bg_copy().wait_send()
    for d in range(1, head_count):
        norm_copy(d).wait_send()
    for bit in range(levels):
        gain_copy(bit).wait_send()
    if levels > 1:
        e_copy().wait_send()

        @pl.loop(0, hh)
        def _(i):
            half_copy(own_start + i).wait_send()
            for bit in range(1, levels):
                link_copy(bit, i, mates[bit]).wait_send()
                pass_copy(bit, own_start + i).wait_send()
                d_copy(bit, i, mates[bit]).wait_send()


def copy_kernel(*refs):
    count = len(refs) // 2
    sems = refs[-1]
    copies = [pltpu.make_async_copy(refs[at], refs[count + at], sems.at[at]) for at in range(count)]
    for copy in copies:
        copy.start()
    for copy in copies:
        copy.wait()


def local(levels, head_count, queries, keys, values, log_decay, level_weight, gate_input, norm_gain, out_grad):
    heads, width, state = queries.shape
    feature = values.shape[2]
    hf, hh = width // 2, heads // 2
    total = heads * head_count * feature
    tokens = jax.ShapeDtypeStruct(queries.shape, BF16)
    vmem = pl.BlockSpec(memory_space=pltpu.VMEM)

    def f32(*shape):
        return pltpu.VMEM(shape, F32)

    def bf16(*shape):
        return pltpu.VMEM(shape, BF16)

    dma = pltpu.SemaphoreType.DMA
    more = max(levels - 1, 1)
    scratch = [
        bf16(heads, width, state), bf16(heads, width, feature),
        f32(heads, width, state), f32(heads, width, feature), f32(heads, width, feature),
        bf16(heads, width, state), f32(heads, width), f32(level_weight.shape[1], heads, width),
        bf16(heads, width, feature), f32(heads, feature), bf16(heads, width, feature),
        f32(heads, 1, width), f32(heads, 1, width), f32(heads, width, hf),
        pltpu.VMEM((hf, hf), jnp.int32),
        f32(levels, heads, state + PAD, feature), f32(levels, heads, state + PAD, feature),
        f32(heads, 3, hf, hf), f32(heads, 3, hf, hf), bf16(heads, width, width),
        bf16(heads, levels * state, width), f32(heads, state, width),
        f32(heads, width, feature), bf16(heads, levels * state, feature), f32(levels, heads, 1, feature),
        f32(2, width, feature), f32(8, width), f32(max(head_count - 1, 1), 8, width),
        f32(2, width, feature), bf16(heads, width, feature),
        f32(heads, more, state, feature), f32(hh, more, state, feature),
        f32(heads, state, feature), f32(heads, state, feature),
        f32(levels, hh, state, feature), f32(levels, hh, state, feature), f32(hh, state, feature),
        f32(heads, state, feature),
        f32(levels, heads, feature), f32(levels, heads, feature),
        dma((8,)),
        dma((levels, heads)), dma((levels, heads)), dma((levels, heads)),
        dma((max(head_count - 1, 1),)), dma((max(head_count - 1, 1),)), dma, dma, dma, dma,
        dma((levels, hh)), dma((levels, hh)), dma((heads,)), dma((heads,)), dma((levels,)), dma((levels,)),
    ]
    hbm = pl.BlockSpec(memory_space=pltpu.HBM)
    turned = jax.ShapeDtypeStruct((level_weight.shape[1], heads, width), F32)
    gains = jax.ShapeDtypeStruct(norm_gain.shape, F32)
    shapes = (tokens, tokens, tokens, tokens, turned, tokens, gains)
    outs = pl.pallas_call(
        functools.partial(kernel, levels, head_count, total),
        out_shape=shapes,
        in_specs=[hbm] * 8,
        out_specs=(vmem,) * 7,
        scratch_shapes=scratch,
        compiler_params=pltpu.CompilerParams(
            collective_id=0, has_side_effects=True, vmem_limit_bytes=52224 * 1024
        ),
    )(
        queries, keys, values, log_decay, jnp.transpose(level_weight, (1, 0, 2)), gate_input, norm_gain, out_grad
    )
    lo, gq, gk, gv, gl, gz, gg = pl.pallas_call(
        copy_kernel,
        out_shape=shapes,
        in_specs=[vmem] * 7,
        out_specs=(hbm,) * 7,
        scratch_shapes=[dma((7,))],
    )(*outs)
    return lo, gq, gk, gv, jnp.transpose(gl, (1, 0, 2)), gz, gg


def solution(mesh):
    levels = mesh.shape["seq"].bit_length() - 1
    tokens = P("head", "seq", None)
    in_specs = (tokens, tokens, tokens, P("head", "seq"), P("head", None, "seq"), tokens, P("head", None), tokens)
    out_specs = (tokens, tokens, tokens, tokens, P("head", None, "seq"), tokens, P("head", None))
    return jax.shard_map(
        functools.partial(local, levels, mesh.shape["head"]),
        mesh=mesh, in_specs=in_specs, out_specs=out_specs, check_vma=False,
    )
```

```python
import functools

import jax
import jax.numpy as jnp
from jax import lax
from jax.experimental import pallas as pl
from jax.experimental.pallas import tpu as pltpu
from jax.sharding import PartitionSpec as P

EPSILON = 1e-05
HIGH = lax.Precision.HIGHEST
F32 = jnp.float32
BF16 = jnp.bfloat16
PAD = 8


def nn(a, b, precision=None):
    return lax.dot_general(a, b, (((1,), (0,)), ((), ())), precision=precision, preferred_element_type=F32)


def nt(a, b, precision=None):
    return lax.dot_general(a, b, (((1,), (1,)), ((), ())), precision=precision, preferred_element_type=F32)


def tn(a, b, precision=None):
    return lax.dot_general(a, b, (((0,), (0,)), ((), ())), precision=precision, preferred_element_type=F32)


def kernel(
    levels, head_count, total,
    q_in, k_in, v_in, ld_in, lw_in, z_in, gain_in, dy_in,
    lo_ref, gq_ref, gk_ref, gv_ref, gl_ref, gz_ref, gg_ref,
    k_ref, v_ref, gkin_s, gvin_s, tailc_s, q_ref, ld_ref, lw_ref, z_ref, gain_ref, dy_ref,
    run_s, tail_s, runc_s, lev_s, own_s, oth_s, w_s, sd_s, mt_s, qst_s, qt_s,
    mixed_s, bks_s, taken_s, acc_s, nsend_s, nrecv_s, col_s, gx_s,
    e_s, er_s, bg_s, bgr_s, dmsg_s, dr_s, d_s, dfull_s, gsend_s, grecv_s,
    in_sem,
    a_send, a_recv, f_send, n_send, n_recv, e_send, e_recv, b_send, b_recv,
    d_send, d_recv, h_send, h_recv, g_send, g_recv,
):
    heads, width, state = q_ref.shape
    hf = width // 2
    hh = heads // 2
    depth = width.bit_length() - 1
    me = lax.axis_index("seq")
    zed = lax.axis_index("head")
    core = me % 2

    def flip(bit):
        step = 1 << bit
        return me + step - 2 * step * ((me // step) % 2)

    def upper(bit):
        return (me // (1 << bit)) % 2 == 1

    mates = [flip(bit) for bit in range(levels)]
    sibling = mates[0]
    own_start = core * hh
    other_start = hh - own_start

    def rcopy(src, dst, ssem, rsem, target):
        return pltpu.make_async_remote_copy(
            src_ref=src, dst_ref=dst, send_sem=ssem, recv_sem=rsem,
            device_id=target, device_id_type=pl.DeviceIdType.MESH,
        )

    def state_copy(start, half):
        part = pl.ds(start, hh)
        return rcopy(own_s.at[0, part], oth_s.at[0, part], a_send.at[0, half], a_recv.at[0, half], {"seq": sibling})

    def link_copy(bit, i, target):
        h = own_start + i
        return rcopy(own_s.at[bit, h], oth_s.at[bit, h], a_send.at[bit, h], a_recv.at[bit, h], {"seq": target})

    def pass_copy(bit, h):
        return rcopy(oth_s.at[bit, h], oth_s.at[bit, h], f_send.at[bit, h], a_recv.at[bit, h], {"seq": sibling})

    def norm_copy(d):
        peer = lax.rem(zed + d, head_count)
        return rcopy(nsend_s, nrecv_s.at[d - 1], n_send.at[d - 1], n_recv.at[d - 1], {"head": peer})

    def e_copy():
        return rcopy(e_s.at[pl.ds(other_start, hh)], er_s, e_send, e_recv, {"seq": sibling})

    def bg_copy():
        return rcopy(bg_s, bgr_s, b_send, b_recv, {"seq": sibling})

    def d_copy(bit, i, target):
        return rcopy(dmsg_s.at[bit, i], dr_s.at[bit, i], d_send.at[bit, i], d_recv.at[bit, i], {"seq": target})

    def half_copy(h):
        return rcopy(dfull_s.at[h], dfull_s.at[h], h_send.at[h], h_recv.at[h], {"seq": sibling})

    def gain_copy(bit):
        return rcopy(gsend_s.at[bit], grecv_s.at[bit], g_send.at[bit], g_recv.at[bit], {"seq": mates[bit]})

    loads = [
        pltpu.make_async_copy(src, dst, in_sem.at[at])
        for at, (src, dst) in enumerate(
            [(ld_in, ld_ref), (k_in, k_ref), (v_in, v_ref), (q_in, q_ref), (lw_in, lw_ref),
             (z_in, z_ref), (dy_in, dy_ref), (gain_in, gain_ref)]
        )
    ]
    for load in loads:
        load.start()
    group = 2 if hh % 2 == 0 else 1

    def together(work, places):
        for store in [work(place) for place in places]:
            store()

    def sweep(work, start, count):
        @pl.loop(0, count // group)
        def _(i):
            together(work, [start + group * i + n for n in range(group)])

    barrier = pltpu.get_barrier_semaphore()
    for mate in mates:
        pl.semaphore_signal(barrier, inc=1, device_id={"seq": mate}, device_id_type=pl.DeviceIdType.MESH)
    for d in range(1, head_count):
        peer = lax.rem(zed + d, head_count)
        pl.semaphore_signal(barrier, inc=1, device_id={"head": peer}, device_id_type=pl.DeviceIdType.MESH)

    loads[0].wait()

    low = lax.broadcasted_iota(jnp.int32, (width, width), 0)
    high = lax.broadcasted_iota(jnp.int32, (width, width), 1)
    running = nn(ld_ref[...], jnp.where(low <= high, 1.0, 0.0), HIGH)
    ending = jnp.broadcast_to(running[:, width - 1 : width], (heads, width))
    tail = jnp.exp(ending - running)
    running_c = running.T
    tail_c = tail.T
    for h in range(heads):
        run_s[h] = running[h : h + 1]
        tail_s[h] = tail[h : h + 1]
        runc_s[h] = jnp.broadcast_to(running_c[:, h : h + 1], (width, hf))
        tailc_s[h] = jnp.broadcast_to(tail_c[:, h : h + 1], (width, hf))
        own_s[0, h, state:] = jnp.broadcast_to(ending[h : h + 1, :hf], (PAD, hf))

    row = lax.broadcasted_iota(jnp.int32, (hf, hf), 0)
    column = lax.broadcasted_iota(jnp.int32, (hf, hf), 1)
    crossed = jnp.bitwise_xor(row, column)
    level = jnp.zeros((hf, hf), jnp.int32)
    for shift in range(depth - 1):
        level = level + jnp.where(crossed >= (1 << shift), 1, 0)
    lev_s[...] = jnp.where(row <= column, level, -1)
    acc_s[...] = jnp.zeros_like(acc_s)

    def own_state(h):
        scaled = (k_ref[h].astype(F32) * tailc_s[h]).astype(BF16)
        summed = tn(scaled, v_ref[h])

        def store():
            own_s[0, h, :state] = summed

        return store

    loads[1].wait()
    loads[2].wait()
    sweep(own_state, other_start, hh)
    pl.semaphore_wait(barrier, levels + head_count - 1)
    state_copy(other_start, 0).start()

    sweep(own_state, own_start, hh)
    state_copy(own_start, 1).start()
    loads[3].wait()
    loads[4].wait()

    def forward(h):
        q, k, v = q_ref[h], k_ref[h], v_ref[h]
        run, runc = run_s[h], runc_s[h]
        lw = [lw_ref[step, pl.ds(h, 1), :] for step in range(depth + 1 + levels)]
        lev = lev_s[...]
        top = nt(k[:hf], q)
        low_scores = nt(k[hf:], q[hf:])

        def diagonal(scores, lo):
            spread = jnp.where(lev >= 0, run[:, lo : lo + hf] - runc[lo : lo + hf], 0.0)
            decay = jnp.exp(spread)
            chosen = jnp.where(lev == 0, lw[0][:, lo : lo + hf], 0.0)
            for step in range(1, depth):
                chosen = jnp.where(lev == step, lw[step][:, lo : lo + hf], chosen)
            weight = decay * chosen
            return weight, scores * decay, (scores * weight).astype(BF16)

        first = diagonal(top[:, :hf], 0)
        last = diagonal(low_scores, hf)
        decay = jnp.exp(run[:, hf:] - runc[:hf])
        weight = decay * lw[depth][:, hf:]
        scores = top[:, hf:]
        corner = weight, scores * decay, (scores * weight).astype(BF16)
        mt = jnp.concatenate(
            [
                jnp.concatenate([first[2], corner[2]], axis=1),
                jnp.concatenate([jnp.zeros((hf, hf), BF16), last[2]], axis=1),
            ],
            axis=0,
        )
        mixed = tn(mt, v)
        qt = q.astype(F32).T
        exp_run = jnp.exp(run)
        scaled = [(qt * (lw[depth + 1 + bit] * exp_run)).astype(BF16) for bit in range(levels)]

        def store():
            for place, part in enumerate((first, corner, last)):
                w_s[h, place] = part[0]
                sd_s[h, place] = part[1]
            mt_s[h] = mt
            mixed_s[h] = mixed
            qt_s[h] = qt
            for bit in range(levels):
                qst_s[h, bit * state : (bit + 1) * state] = scaled[bit]

        return store

    def merge(bit, i):
        h = own_start + i
        mine, theirs = own_s[bit, h], oth_s[bit, h]
        own_rate, other_rate = mine[state : state + 1], theirs[state : state + 1]
        own_f = jnp.where(upper(bit), 1.0, jnp.exp(other_rate))
        other_f = jnp.where(upper(bit), jnp.exp(own_rate), 1.0)
        own_s[bit + 1, h, :state] = own_f * mine[:state] + other_f * theirs[:state]
        own_s[bit + 1, h, state:] = mine[state:] + theirs[state:]

    together(forward, range(group))
    done = group
    state_copy(own_start, 0).wait_recv()
    state_copy(own_start, 1).wait_recv()
    if levels > 1:

        @pl.loop(0, hh)
        def _(i):
            merge(0, i)
            link_copy(1, i, mates[1]).start()

    for bit in range(1, levels - 1):
        if done + group <= heads:
            together(forward, range(done, done + group))
            done += group
        ahead_of = min(heads - done, hh)

        @pl.loop(0, hh // group)
        def _(j, bit=bit, done=done, ahead_of=ahead_of):
            for n in range(group):
                i = group * j + n
                link_copy(bit, i, mates[bit]).wait_recv()
                merge(bit, i)
                link_copy(bit + 1, i, mates[bit + 1]).start()
                pass_copy(bit, own_start + i).start()

            @pl.when(group * j < ahead_of)
            def _():
                together(forward, [done + group * j + n for n in range(group)])

        done += ahead_of

    if done < heads:
        sweep(forward, done, heads - done)

    def outer(h):
        ahead = jnp.zeros((1, state), F32)
        shares, buckets = [], []
        for bit in range(levels):
            taken = jnp.where(upper(bit), jnp.exp(ahead), 0.0)
            shares.append(taken)
            buckets.append((taken * oth_s[bit, h, :state]).astype(BF16))
            ahead = ahead + jnp.where(upper(bit), oth_s[bit, h, state : state + 1], 0.0)
        mixed = mixed_s[h] + tn(qst_s[h], jnp.concatenate(buckets, axis=0))
        z = z_ref[h].astype(F32)
        gated = mixed * (z * jax.nn.sigmoid(z))
        scaled = dy_ref[h].astype(F32) * gain_ref[pl.ds(h, 1), :]

        def store():
            for bit in range(levels):
                taken_s[bit, h] = shares[bit]
                bks_s[h, bit * state : (bit + 1) * state] = buckets[bit]
            mixed_s[h] = mixed
            acc_s[0] += gated * gated
            acc_s[1] += gated * scaled

        return store

    for load in loads[5:]:
        load.wait()

    @pl.loop(0, hh // group)
    def _(j):
        places = [own_start + group * j + n for n in range(group)]
        if levels > 1:
            for n in range(group):
                link_copy(levels - 1, group * j + n, mates[levels - 1]).wait_recv()
                pass_copy(levels - 1, places[n]).start()
        together(outer, places)

    @pl.loop(0, hh // group)
    def _(j):
        places = [other_start + group * j + n for n in range(group)]
        for h in places:
            for bit in range(1, levels):
                pass_copy(bit, h).wait_recv()
        together(outer, places)

    pick = lax.broadcasted_iota(jnp.int32, (8, state), 0)
    sums = nt(jnp.where(pick == 0, 1.0, 0.0), acc_s[0], HIGH) + nt(jnp.where(pick == 1, 1.0, 0.0), acc_s[1], HIGH)
    nsend_s[...] = sums
    for d in range(1, head_count):
        norm_copy(d).start()
    for d in range(1, head_count):
        norm_copy(d).wait_recv()
        sums = sums + nrecv_s[d - 1]
    inverse = lax.rsqrt(sums[0:1] / total + EPSILON)
    pull = inverse * inverse * inverse * sums[1:2] / total
    columns = jnp.where(lax.broadcasted_iota(jnp.int32, (8, width), 0) == 0, inverse, pull).T
    col_s[0] = jnp.broadcast_to(columns[:, 0:1], (width, state))
    col_s[1] = jnp.broadcast_to(columns[:, 1:2], (width, state))

    def gate_back(h):
        z = z_ref[h].astype(F32)
        sig = jax.nn.sigmoid(z)
        act = z * sig
        mixed = mixed_s[h]
        gated = mixed * act
        gain = gain_ref[pl.ds(h, 1), :]
        dy = dy_ref[h].astype(F32)
        inv = col_s[0]
        normed = gated * inv
        shown = (gain * normed).astype(BF16)
        gain_sum = jnp.sum(dy * normed, axis=0, keepdims=True)
        grad = inv * (dy * gain) - gated * col_s[1]
        gz = (grad * mixed * sig * (1.0 + z * (1.0 - sig))).astype(BF16)
        gx = (grad * act).astype(BF16)
        grads = nn(qst_s[h], gx)
        parts = [taken_s[bit, h] * grads[bit * state : (bit + 1) * state] for bit in range(levels)]

        def store():
            lo_ref[h] = shown
            gsend_s[0, pl.ds(h, 1), :] = gain_sum
            gz_ref[h] = gz
            gx_s[h] = gx
            bg_s[h] = parts[0]
            for bit in range(1, levels):
                e_s[h, bit - 1] = parts[bit]

        return store

    sweep(gate_back, other_start, hh)
    if levels > 1:
        e_copy().start()

    def send_down(bit, i):
        h = own_start + i
        e = e_s[h, bit - 1] + er_s[i, bit - 1]
        if bit < levels - 1:
            rate, other_rate = own_s[bit, h, state : state + 1], oth_s[bit, h, state : state + 1]
            other_f = jnp.where(upper(bit), jnp.exp(rate), 1.0)
            e = e + other_f * d_s[i]
        dmsg_s[bit, i] = e
        d_copy(bit, i, mates[bit]).start()

    def take_down(bit, i):
        h = own_start + i
        d_copy(bit, i, mates[bit]).wait_recv()
        got = dr_s[bit, i]
        if bit < levels - 1:
            other_rate = oth_s[bit, h, state : state + 1]
            own_f = jnp.where(upper(bit), 1.0, jnp.exp(other_rate))
            got = got + own_f * d_s[i]
        if bit > 1:
            d_s[i] = got
        else:
            dfull_s[h] = got

    @pl.loop(0, hh // group)
    def _(j):
        together(gate_back, [own_start + group * j + n for n in range(group)])
        if levels > 1:

            @pl.when(j == 0)
            def _():
                e_copy().wait_recv()

            for n in range(group):
                send_down(levels - 1, group * j + n)

    bg_copy().start()
    gain_copy(0).start()
    if levels == 1:
        dfull_s[...] = jnp.zeros_like(dfull_s)

    def block_grads(h):
        q, k, v, gx = q_ref[h], k_ref[h], v_ref[h], gx_s[h]
        lev = lev_s[...]
        top = nt(v[:hf], gx)
        low_grads = nt(v[hf:], gx[hf:])
        parts = ((top[:, :hf], 0), (top[:, hf:], hf), (low_grads, hf))
        spread = [(part * w_s[h, place]).astype(BF16) for place, (part, lo) in enumerate(parts)]
        gst = jnp.concatenate(
            [
                jnp.concatenate([spread[0], spread[1]], axis=1),
                jnp.concatenate([jnp.zeros((hf, hf), BF16), spread[2]], axis=1),
            ],
            axis=0,
        )
        moved = [parts[place][0] * sd_s[h, place] for place in (0, 2)]
        rows = [
            jnp.concatenate(
                [jnp.sum(jnp.where(lev == step, part, 0.0), axis=0, keepdims=True) for part in moved], axis=1
            )
            for step in range(depth)
        ]
        corner = jnp.sum(top[:, hf:] * sd_s[h, 1], axis=0, keepdims=True)
        rows.append(jnp.concatenate([jnp.zeros((1, hf), F32), corner], axis=1))
        gkin = nn(gst, q)
        gvin = nn(mt_s[h], gx)
        gqt = tn(k, gst)
        pulled = nt(bks_s[h], gx)
        exp_run = jnp.exp(run_s[h])
        qt = qt_s[h]
        outs = []
        for bit in range(levels):
            here = pulled[bit * state : (bit + 1) * state]
            outs.append(exp_run * jnp.sum(qt * here, axis=0, keepdims=True))
            gqt = gqt + (lw_ref[depth + 1 + bit, pl.ds(h, 1), :] * exp_run) * here
        gq = gqt.T.astype(BF16)

        def store():
            here = lax.broadcasted_iota(jnp.int32, (heads, width), 0) == h
            for step, line in enumerate(rows + outs):
                gl_ref[step] = jnp.where(here, line, gl_ref[step])
            gkin_s[h] = gkin
            gvin_s[h] = gvin
            gq_ref[h] = gq

        return store

    def finish(h):
        own_f = jnp.where(upper(0), 1.0, jnp.exp(oth_s[0, h, state : state + 1]))
        down = (own_f * dfull_s[h] + bgr_s[h]).astype(BF16)
        tail = tailc_s[h]
        gk = (gkin_s[h] + tail * nt(v_ref[h], down)).astype(BF16)
        gv = (gvin_s[h] + tail * nn(k_ref[h], down)).astype(BF16)

        def store():
            gk_ref[h] = gk
            gv_ref[h] = gv

        return store

    gl_ref[...] = jnp.zeros_like(gl_ref)
    done = 0
    for bit in range(levels - 1, 1, -1):
        if done + group <= heads:
            together(block_grads, range(done, done + group))
            done += group
        ahead_of = min(heads - done, hh)
        turn = levels - 1 - bit
        gain_copy(turn).wait_recv()
        gsend_s[turn + 1] = gsend_s[turn] + grecv_s[turn]
        gain_copy(turn + 1).start()

        @pl.loop(0, hh // group)
        def _(j, bit=bit, done=done, ahead_of=ahead_of):
            for n in range(group):
                i = group * j + n
                take_down(bit, i)
                send_down(bit - 1, i)

            @pl.when(group * j < ahead_of)
            def _():
                together(block_grads, [done + group * j + n for n in range(group)])

        done += ahead_of

    if done < heads:
        sweep(block_grads, done, heads - done)
    if levels > 1:
        turn = levels - 2
        gain_copy(turn).wait_recv()
        gsend_s[turn + 1] = gsend_s[turn] + grecv_s[turn]
        gain_copy(turn + 1).start()
    bg_copy().wait_recv()

    @pl.loop(0, hh // group)
    def _(j):
        places = [group * j + n for n in range(group)]
        if levels > 1:
            for i in places:
                take_down(1, i)
                half_copy(own_start + i).start()
        together(finish, [own_start + i for i in places])

    @pl.loop(0, hh // group)
    def _(j):
        places = [other_start + group * j + n for n in range(group)]
        if levels > 1:
            for h in places:
                half_copy(h).wait_recv()
        together(finish, places)

    gain_copy(levels - 1).wait_recv()
    gg_ref[...] = gsend_s[levels - 1] + grecv_s[levels - 1]
    state_copy(other_start, 0).wait_send()
    state_copy(own_start, 1).wait_send()
    bg_copy().wait_send()
    for d in range(1, head_count):
        norm_copy(d).wait_send()
    for bit in range(levels):
        gain_copy(bit).wait_send()
    if levels > 1:
        e_copy().wait_send()

        @pl.loop(0, hh)
        def _(i):
            half_copy(own_start + i).wait_send()
            for bit in range(1, levels):
                link_copy(bit, i, mates[bit]).wait_send()
                pass_copy(bit, own_start + i).wait_send()
                d_copy(bit, i, mates[bit]).wait_send()


def copy_kernel(*refs):
    count = len(refs) // 2
    sems = refs[-1]
    copies = [pltpu.make_async_copy(refs[at], refs[count + at], sems.at[at]) for at in range(count)]
    for copy in copies:
        copy.start()
    for copy in copies:
        copy.wait()


def local(levels, head_count, queries, keys, values, log_decay, level_weight, gate_input, norm_gain, out_grad):
    heads, width, state = queries.shape
    feature = values.shape[2]
    hf, hh = width // 2, heads // 2
    total = heads * head_count * feature
    tokens = jax.ShapeDtypeStruct(queries.shape, BF16)
    vmem = pl.BlockSpec(memory_space=pltpu.VMEM)

    def f32(*shape):
        return pltpu.VMEM(shape, F32)

    def bf16(*shape):
        return pltpu.VMEM(shape, BF16)

    dma = pltpu.SemaphoreType.DMA
    more = max(levels - 1, 1)
    scratch = [
        bf16(heads, width, state), bf16(heads, width, feature),
        f32(heads, width, state), f32(heads, width, feature), f32(heads, width, feature),
        bf16(heads, width, state), f32(heads, width), f32(level_weight.shape[1], heads, width),
        bf16(heads, width, feature), f32(heads, feature), bf16(heads, width, feature),
        f32(heads, 1, width), f32(heads, 1, width), f32(heads, width, hf),
        pltpu.VMEM((hf, hf), jnp.int32),
        f32(levels, heads, state + PAD, feature), f32(levels, heads, state + PAD, feature),
        f32(heads, 3, hf, hf), f32(heads, 3, hf, hf), bf16(heads, width, width),
        bf16(heads, levels * state, width), f32(heads, state, width),
        f32(heads, width, feature), bf16(heads, levels * state, feature), f32(levels, heads, 1, feature),
        f32(2, width, feature), f32(8, width), f32(max(head_count - 1, 1), 8, width),
        f32(2, width, feature), bf16(heads, width, feature),
        f32(heads, more, state, feature), f32(hh, more, state, feature),
        f32(heads, state, feature), f32(heads, state, feature),
        f32(levels, hh, state, feature), f32(levels, hh, state, feature), f32(hh, state, feature),
        f32(heads, state, feature),
        f32(levels, heads, feature), f32(levels, heads, feature),
        dma((8,)),
        dma((levels, heads)), dma((levels, heads)), dma((levels, heads)),
        dma((max(head_count - 1, 1),)), dma((max(head_count - 1, 1),)), dma, dma, dma, dma,
        dma((levels, hh)), dma((levels, hh)), dma((heads,)), dma((heads,)), dma((levels,)), dma((levels,)),
    ]
    hbm = pl.BlockSpec(memory_space=pltpu.HBM)
    turned = jax.ShapeDtypeStruct((level_weight.shape[1], heads, width), F32)
    gains = jax.ShapeDtypeStruct(norm_gain.shape, F32)
    shapes = (tokens, tokens, tokens, tokens, turned, tokens, gains)
    outs = pl.pallas_call(
        functools.partial(kernel, levels, head_count, total),
        out_shape=shapes,
        in_specs=[hbm] * 8,
        out_specs=(vmem,) * 7,
        scratch_shapes=scratch,
        compiler_params=pltpu.CompilerParams(
            collective_id=0, has_side_effects=True, vmem_limit_bytes=51680 * 1024
        ),
    )(
        queries, keys, values, log_decay, jnp.transpose(level_weight, (1, 0, 2)), gate_input, norm_gain, out_grad
    )
    lo, gq, gk, gv, gl, gz, gg = pl.pallas_call(
        copy_kernel,
        out_shape=shapes,
        in_specs=[vmem] * 7,
        out_specs=(hbm,) * 7,
        scratch_shapes=[dma((7,))],
    )(*outs)
    return lo, gq, gk, gv, jnp.transpose(gl, (1, 0, 2)), gz, gg


def solution(mesh):
    levels = mesh.shape["seq"].bit_length() - 1
    tokens = P("head", "seq", None)
    in_specs = (tokens, tokens, tokens, P("head", "seq"), P("head", None, "seq"), tokens, P("head", None), tokens)
    out_specs = (tokens, tokens, tokens, tokens, P("head", None, "seq"), tokens, P("head", None))
    return jax.shard_map(
        functools.partial(local, levels, mesh.shape["head"]),
        mesh=mesh, in_specs=in_specs, out_specs=out_specs, check_vma=False,
    )
```
